128 devices in a mesh: dp: 8 (over z, core), mp: 16 (over x, y).
Axes of the slice: x: 4, y: 4, z: 4, core: 2. Of those that a mesh axis runs over, the one named last changes fastest.
Arguments:
- gradient: bfloat16 [100663296], P(('dp', 'mp'))
- block_position: int32 [96], replicated, may hold values from 0 to 95, as said below
- block_owner: int32 [96], replicated, may hold values from 0 to 127, as said below
- left_stats: float32 [128, 1024, 1024], P(('dp', 'mp'))
- right_stats: float32 [128, 1024, 1024], P(('dp', 'mp'))
- left_root: bfloat16 [128, 1024, 1024], P(('dp', 'mp'))
- right_root: bfloat16 [128, 1024, 1024], P(('dp', 'mp'))
Outputs:
- update: bfloat16 [100663296], P(('dp', 'mp'))
- new_left: float32 [128, 1024, 1024], P(('dp', 'mp'))
- new_right: float32 [128, 1024, 1024], P(('dp', 'mp'))
The draws below stay inside these ranges and needn't reach their ends.
Inputs may be any that keep to these rules, and one draw needn't show every extreme that they name: `block_position`: a permutation of the block numbers. `block_owner`: all owners differ; the owner of the block at position p is one of the devices 4 * (p // 3) to 4 * (p // 3) + 3; devices 0 and 128 - 1 always own a block.
All inputs are finite; a program needn't handle non-finite values.
Results may differ from the reference program's by a relative error of at most 0.0057.
Values may be sent and summed in bfloat16 or wider, within the bound.
A program may use at most 128 MiB of HBM per device.

```python
import jax
import jax.numpy as jnp
from jax import lax

B = 1024
BLOCKS = 96
FLAT = 100663296
DEVICES = 128


def block_layout(key):
    order = jax.random.permutation(jax.random.fold_in(key, 101), BLOCKS).astype(jnp.int32)
    groups = BLOCKS // 3
    dropped = jax.random.randint(jax.random.fold_in(key, 103), (groups,), 0, 4).astype(jnp.int32)
    dropped = dropped.at[0].set(1 + dropped[0] % 3)
    dropped = dropped.at[groups - 1].set(dropped[groups - 1] % 3)
    columns = jnp.arange(4, dtype=jnp.int32)[None, :]
    scores = jax.random.randint(jax.random.fold_in(key, 102), (groups, 4), 0, 1 << 20) * 4 + columns
    scores = scores + jnp.where(columns == dropped[:, None], 1 << 23, 0).astype(jnp.int32)
    ranked = jnp.argsort(scores, axis=1).astype(jnp.int32)
    owner_of_place = (4 * jnp.arange(groups, dtype=jnp.int32)[:, None] + ranked[:, :3]).reshape(BLOCKS)
    return (order, owner_of_place[order])


def draw_block_position(key, part):
    order, owners = block_layout(key)
    return order


def draw_block_owner(key, part):
    order, owners = block_layout(key)
    return owners


def draw_gradient(key, part):
    key = jax.random.fold_in(key, 3)
    place = jnp.arange(FLAT, dtype=jnp.float32) / FLAT
    rising = jnp.exp(jnp.log(3.0) * place)
    values = jax.random.normal(jax.random.fold_in(key, 7), (FLAT,), jnp.float32) * rising
    return jnp.clip(values, -12.0, 12.0).astype(jnp.bfloat16)


def symmetric_slots(key, lowest, highest, spread):
    slot_scale = jax.random.uniform(jax.random.fold_in(key, 11), (DEVICES, 1, 1), jnp.float32, jnp.log(lowest), jnp.log(highest))
    diag_scale = jax.random.uniform(jax.random.fold_in(key, 12), (DEVICES, B), jnp.float32, jnp.log(0.5), jnp.log(2.0))
    diagonal = jnp.exp(diag_scale)
    raw = jax.random.normal(jax.random.fold_in(key, 13), (DEVICES, B, B), jnp.float32)
    offdiag = (raw + jnp.swapaxes(raw, 1, 2)) * (spread / jnp.sqrt(2.0 * B))
    eye = jnp.eye(B, dtype=jnp.float32)[None, :, :]
    return jnp.exp(slot_scale) * (diagonal[:, :, None] * eye + offdiag)


def draw_left_stats(key, part):
    key = jax.random.fold_in(key, 21)
    return symmetric_slots(key, 0.5, 2.0, 0.5)


def draw_right_stats(key, part):
    key = jax.random.fold_in(key, 22)
    return symmetric_slots(key, 0.5, 2.0, 0.5)


def draw_left_root(key, part):
    key = jax.random.fold_in(key, 23)
    return symmetric_slots(key, 0.5, 2.0, 0.4).astype(jnp.bfloat16)


def draw_right_root(key, part):
    key = jax.random.fold_in(key, 24)
    return symmetric_slots(key, 0.5, 2.0, 0.4).astype(jnp.bfloat16)


def setup_inputs(seed: int = 0) -> dict:
    splits = jax.random.split(jax.random.key(seed), 8)
    gradient = draw_gradient(jax.random.fold_in(splits[7], 71), 0)
    block_position = draw_block_position(jax.random.fold_in(splits[7], 71), 0)
    block_owner = draw_block_owner(jax.random.fold_in(splits[7], 71), 0)
    left_stats = draw_left_stats(jax.random.fold_in(splits[7], 71), 0)
    right_stats = draw_right_stats(jax.random.fold_in(splits[7], 71), 0)
    left_root = draw_left_root(jax.random.fold_in(splits[7], 71), 0)
    right_root = draw_right_root(jax.random.fold_in(splits[7], 71), 0)
    return dict(gradient=gradient, block_position=block_position, block_owner=block_owner, left_stats=left_stats, right_stats=right_stats, left_root=left_root, right_root=right_root)


DECAY_RATE = 0.95
EPSILON = 1e-06

def reference(gradient, block_position, block_owner, left_stats, right_stats, left_root, right_root):
    blocks = gradient.reshape(BLOCKS, B, B)
    slot_position = jnp.full((DEVICES,), -1, jnp.int32).at[block_owner.astype(jnp.int32)].set(block_position.astype(jnp.int32))

    def per_slot(inputs_one):
        place, old_left, old_right, root_left, root_right = inputs_one
        chosen = lax.dynamic_index_in_dim(blocks, jnp.maximum(place, 0).astype(jnp.int32), 0, keepdims=False)
        grad_block = jnp.where(place >= 0, chosen, jnp.zeros((B, B), jnp.bfloat16))
        gram_left = jnp.dot(grad_block, grad_block.T, preferred_element_type=jnp.float32)
        gram_right = jnp.dot(grad_block.T, grad_block, preferred_element_type=jnp.float32)
        fresh_left = DECAY_RATE * old_left + (1.0 - DECAY_RATE) / B * gram_left
        fresh_right = DECAY_RATE * old_right + (1.0 - DECAY_RATE) / B * gram_right
        left_half = jnp.dot(root_left, grad_block, preferred_element_type=jnp.float32).astype(jnp.bfloat16)
        direction = jnp.dot(left_half, root_right, preferred_element_type=jnp.float32).astype(jnp.bfloat16)
        return (fresh_left, fresh_right, direction)
    new_left, new_right, directions = lax.map(per_slot, (slot_position, left_stats, right_stats, left_root, right_root))
    target = jnp.where(slot_position >= 0, slot_position, BLOCKS).astype(jnp.int32)
    flat_direction = jnp.zeros((BLOCKS, B, B), jnp.bfloat16).at[target].set(directions, mode='drop')
    grad_square = jnp.sum(jnp.square(gradient.astype(jnp.float32)))
    direction_square = jnp.sum(jnp.square(flat_direction.astype(jnp.float32)))
    graft_scale = jnp.sqrt(grad_square / (direction_square + EPSILON))
    update = (graft_scale * flat_direction.astype(jnp.float32)).astype(jnp.bfloat16).reshape(FLAT)
    return (update, new_left, new_right)
```

```python
import functools
import itertools

import jax
import jax.numpy as jnp
import numpy as np
from jax import lax
from jax.experimental import pallas as pl
from jax.experimental.pallas import tpu as pltpu
from jax.sharding import PartitionSpec as P

DECAY_RATE = 0.95
EPSILON = 1e-06
MESH = pl.DeviceIdType.MESH

RING = 4
GROUP_BLOCKS = 3
B = 1024
PIECE = 128
HELD = 6
OWNED = B // PIECE
COLS = 256
QUARTERS = B // COLS
SLOTS = 6
EARLY = 3
EARLIER = B - COLS
WORDS = 8
LANES = 128
SUBROWS = B // LANES
F32, BF16 = jnp.float32, jnp.bfloat16


def schedule(wanted):
    ways = (1, RING - 1)
    far = [i for i in range(RING) if wanted[i][(i + 2) % RING]]
    best = None
    for split in itertools.product(*[range(len(wanted[i][(i + 2) % RING]) + 1) for i in far]):
        plus = dict(zip(far, split))
        first = {}
        for i in range(RING):
            pieces = wanted[i][(i + 2) % RING]
            n = plus.get(i, 0)
            first[i, 0], first[i, 1] = pieces[:n], pieces[n:]
        if max(len(p) for p in first.values()) > EARLY:
            continue
        loads = [
            len(first[i, w]) + len(first[(i - way) % RING, w]) + len(wanted[i][(i + way) % RING])
            for i in range(RING)
            for w, way in enumerate(ways)
        ]
        key = (max(loads), sum(v * v for v in loads))
        if best is None or key < best[0]:
            best = (key, first)
    assert best is not None and best[0][0] <= SLOTS
    first = best[1]
    sent = {}
    for i in range(RING):
        for w, way in enumerate(ways):
            slots = [None] * SLOTS
            for k, piece in enumerate(first[i, w]):
                slots[k] = ("own", piece)
            for k, piece in enumerate(first[(i - way) % RING, w]):
                slots[EARLY + k] = ("pass", piece)
            free = [t for t in range(SLOTS) if slots[t] is None]
            for t, piece in zip(free, wanted[i][(i + way) % RING]):
                slots[t] = ("own", piece)
            sent[i, w] = slots
    return sent


def packed(codes):
    return sum(int(c) << (5 * k) for k, c in enumerate(codes))


def tables():
    out = np.zeros((RING**GROUP_BLOCKS, RING, WORDS), np.int32)
    for owners in itertools.permutations(range(RING), GROUP_BLOCKS):
        row = (owners[0] * RING + owners[1]) * RING + owners[2]
        there = [[[] for _ in range(RING)] for _ in range(RING)]
        back = [[[] for _ in range(RING)] for _ in range(RING)]
        for piece in range(RING * HELD):
            holder, owner = piece // HELD, owners[piece // OWNED]
            there[holder][owner].append(piece)
            back[owner][holder].append(piece)
        for wanted, size, word in ((there, HELD, 0), (back, OWNED, 4)):
            sent = schedule(wanted)
            for i in range(RING):
                for w in range(2):
                    codes = []
                    for entry in sent[i, w]:
                        if entry is None:
                            codes.append(0)
                        elif entry[0] == "own":
                            codes.append(entry[1] % size)
                        else:
                            codes.append(size)
                    out[row, i, word + w] = packed(codes)
                arrived = {}
                for w, way in enumerate((1, RING - 1)):
                    for t, entry in enumerate(sent[(i - way) % RING, w]):
                        if entry is not None:
                            arrived[entry[1]] = size + w * SLOTS + t
                if word == 0:
                    codes = [HELD + 2 * SLOTS] * OWNED
                    if i in owners:
                        first = owners.index(i) * OWNED
                        for q in range(OWNED):
                            piece = first + q
                            mine = piece // HELD == i
                            codes[q] = piece % HELD if mine else arrived[piece]
                    out[row, i, 2] = packed(codes[:6])
                    out[row, i, 3] = packed(codes[6:])
                else:
                    codes = []
                    for k in range(HELD):
                        piece = i * HELD + k
                        mine = owners[piece // OWNED] == i
                        codes.append(piece % OWNED if mine else arrived[piece])
                    out[row, i, 6] = packed(codes)
    return out.reshape(-1)


def code(word, k):
    return lax.bitwise_and(lax.shift_right_logical(word, jnp.int32(5 * k)), jnp.int32(31))


def kernel(
    sizes,
    position_in,
    owner_in,
    table_in,
    gradient,
    left_stats,
    right_stats,
    left_root,
    right_root,
    wide,
    scale,
    new_left,
    new_right,
    position,
    owner,
    table,
    flat,
    grads,
    left,
    right,
    half,
    begun,
    own,
    there_out,
    there_in,
    product,
    back_out,
    back_in,
    sums_out,
    sums_in,
    local_sem,
    there_send,
    there_recv,
    back_send,
    back_recv,
    sums_send,
    sums_recv,
):
    xs, ys, zs, cores = sizes
    dp, mp = lax.axis_index("dp"), lax.axis_index("mp")
    z, core = dp // cores, dp % cores
    x, y = mp // ys, mp % ys

    def at(x, y, z, core):
        return (z * cores + core, x * ys + y)

    neighbours = (at(x, (y + 1) % ys, z, core), at(x, (y + ys - 1) % ys, z, core))

    here = (x, y, z, core)
    rounds = [(place, size) for place, size in ((1, ys), (0, xs), (2, zs), (3, cores)) if size > 1]

    def along(place, size, distance):
        there = list(here)
        there[place] = (here[place] + distance) % size
        return at(*there)

    greeted = [along(place, size, d) for place, size in rounds for d in range(1, size)]

    barrier = pltpu.get_barrier_semaphore()
    for device in greeted:
        pl.semaphore_signal(barrier, inc=1, device_id=device, device_id_type=MESH)

    loads = [
        pltpu.make_async_copy(source, target, local_sem.at[k])
        for k, (source, target) in enumerate(
            (
                (gradient, flat),
                (left_root, left),
                (right_root, right),
                (left_stats, new_left),
                (right_stats, new_right),
                (position_in, position),
                (owner_in, owner),
                (table_in, table),
            )
        )
    ]
    for k in (5, 6, 7, 0, 1, 2, 3, 4):
        loads[k].start()

    group = (dp * (xs * ys) + mp) // RING

    def find(b, found):
        place, device = position[b], owner[b]
        return tuple(
            jnp.where(place == GROUP_BLOCKS * group + k, device, f) for k, f in enumerate(found)
        )

    for k in (5, 6, 7):
        loads[k].wait()
    zero = jnp.int32(0)
    found = lax.fori_loop(0, position.shape[0], find, (zero,) * GROUP_BLOCKS)
    row = zero
    for f in found:
        row = row * RING + (f - RING * group)
    row = jnp.clip(row, 0, RING**GROUP_BLOCKS - 1)
    base = (row * RING + y) * WORDS
    words = [table[base + k] for k in range(7)]

    loads[0].wait()
    grad_sum = jnp.zeros((8, LANES), F32)
    rows = PIECE * SUBROWS
    for k in range(HELD):
        values = flat[pl.ds(k * rows, rows), :].astype(F32)
        wide[pl.ds(k * rows, rows), :] = values
        grad_sum += jnp.sum(jnp.square(values).reshape(rows // 8, 8, LANES), axis=0)

    def take(s):
        for k in range(HELD):
            for h in range(COLS // LANES):
                start = k * rows + s * (COLS // LANES) + h
                block = wide[pl.ds(start, PIECE, stride=SUBROWS), :]
                own[s][k, :, h * LANES : (h + 1) * LANES] = block.astype(BF16)

    def copy_of(out, into, send, recv, s, w, late):
        slots = pl.ds(w * SLOTS + late * EARLY, EARLY)
        return pltpu.make_async_remote_copy(
            src_ref=out[s].at[slots],
            dst_ref=into[s].at[slots],
            send_sem=send.at[s],
            recv_sem=recv.at[s, 2 * late + w],
            device_id=neighbours[w],
            device_id_type=MESH,
        )

    def send_own(out, into, send, recv, source, pair, size, s):
        for w in range(2):
            for t in range(EARLY):
                out[s][w * SLOTS + t] = source[s][jnp.minimum(code(pair[w], t), size - 1)]
            copy_of(out, into, send, recv, s, w, 0).start()

    def send_on(out, into, send, recv, source, pair, size, s):
        for w in range(2):
            copy_of(out, into, send, recv, s, w, 0).wait_recv()
            for t in range(EARLY, SLOTS):
                c = code(pair[w], t)
                passed = into[s][w * SLOTS + t - EARLY]
                mine = source[s][jnp.minimum(c, size - 1)]
                out[s][w * SLOTS + t] = jnp.where(c == size, passed, mine)
            copy_of(out, into, send, recv, s, w, 1).start()

    def arrive(out, into, send, recv, s):
        for w in range(2):
            copy_of(out, into, send, recv, s, w, 1).wait_recv()

    def all_sent(out, into, send, recv, s):
        pltpu.make_async_remote_copy(
            src_ref=out[s],
            dst_ref=into[s],
            send_sem=send.at[s],
            recv_sem=recv.at[s, 0],
            device_id=neighbours[0],
            device_id_type=MESH,
        ).wait_send()

    def pick(source, into, c, size, s):
        mine = source[s][jnp.minimum(c, size - 1)]
        came = into[s][jnp.clip(c - size, 0, 2 * SLOTS - 1)]
        return jnp.where(c < size, mine, came)

    there = (there_out, there_in, there_send, there_recv)
    back = (back_out, back_in, back_send, back_recv)

    def there_own(s):
        take(s)
        send_own(*there, own, words[0:2], HELD, s)

    def there_on(s):
        send_on(*there, own, words[0:2], HELD, s)

    def multiply_left(s):
        arrive(*there, s)
        for q in range(OWNED):
            c = code(words[2 + q // 6], q % 6)
            value = pick(own, there_in, c, HELD, s)
            value = jnp.where(c < HELD + 2 * SLOTS, value, jnp.zeros_like(value))
            grads[s, pl.ds(q * PIECE, PIECE), :] = value
        if s == 0:
            loads[1].wait()

        def tile(r, carry):
            at_rows = pl.ds(pl.multiple_of(r * COLS, COLS), COLS)
            part = jnp.dot(left[at_rows, :], grads[s], preferred_element_type=F32)
            half[at_rows, s * COLS : (s + 1) * COLS] = part.astype(BF16)
            return carry

        lax.fori_loop(0, B // COLS, tile, 0)

    def begin_right():
        loads[2].wait()

        def tile(r, carry):
            at_rows = pl.ds(pl.multiple_of(r * COLS, COLS), COLS)
            begun[at_rows, :] = jnp.dot(
                half[at_rows, :EARLIER], right[:EARLIER, :COLS], preferred_element_type=F32
            )
            return carry

        lax.fori_loop(0, B // COLS, tile, 0)

    pl.semaphore_wait(barrier, len(greeted))
    there_own(0)
    there_own(1)
    there_own(2)
    there_on(0)
    there_own(3)
    there_on(1)
    multiply_left(0)
    there_on(2)
    multiply_left(1)
    there_on(3)
    multiply_left(2)
    begin_right()
    multiply_left(3)

    def multiply_right(s, total):
        def tile(r, total):
            at_rows = pl.ds(pl.multiple_of(r * COLS, COLS), COLS)
            at_cols = pl.ds(s * COLS, COLS)
            if s == 0:
                part = jnp.dot(
                    half[at_rows, EARLIER:], right[EARLIER:, at_cols], preferred_element_type=F32
                )
                part = (begun[at_rows, :] + part).astype(BF16)
            else:
                part = jnp.dot(
                    half[at_rows, :], right[:, at_cols], preferred_element_type=F32
                ).astype(BF16)
            product[s][pl.ds(r * 2, 2)] = part.reshape(2, PIECE, COLS)
            squares = jnp.square(part.astype(F32))
            squares = squares[:, :LANES] + squares[:, LANES:]
            return total + jnp.sum(squares.reshape(COLS // 8, 8, LANES), axis=0)

        return lax.fori_loop(0, B // COLS, tile, total)

    def back_own(s):
        send_own(*back, product, words[4:6], OWNED, s)

    def back_on(s):
        send_on(*back, product, words[4:6], OWNED, s)

    def finish(s):
        arrive(*back, s)
        for k in range(HELD):
            value = pick(product, back_in, code(words[6], k), OWNED, s).astype(F32)
            for h in range(COLS // LANES):
                start = k * rows + s * (COLS // LANES) + h
                wide[pl.ds(start, PIECE, stride=SUBROWS), :] = value[:, h * LANES : (h + 1) * LANES]

    def exchange(r, d):
        place, size = rounds[r]
        return pltpu.make_async_remote_copy(
            src_ref=sums_out.at[r],
            dst_ref=sums_in.at[r, here[place]],
            send_sem=sums_send.at[r],
            recv_sem=sums_recv.at[r],
            device_id=along(place, size, d),
            device_id_type=MESH,
        )

    def exchange_start(r, sums):
        place, size = rounds[r]
        sums_out[r] = sums
        for d in range(1, size):
            exchange(r, d).start()

    def exchange_all(r):
        size = rounds[r][1]
        return pltpu.make_async_remote_copy(
            src_ref=sums_in.at[r, pl.ds(0, size - 1)],
            dst_ref=sums_in.at[r, pl.ds(0, size - 1)],
            send_sem=sums_send.at[r],
            recv_sem=sums_recv.at[r],
            device_id=along(*rounds[r], 1),
            device_id_type=MESH,
        )

    def exchange_end(r):
        place, size = rounds[r]
        sums_in[r, here[place]] = sums_out[r]
        exchange_all(r).wait_recv()
        return sum((sums_in[r, k] for k in range(1, size)), sums_in[r, 0])

    def exchange_sent(r):
        exchange_all(r).wait_send()

    factor = (1.0 - DECAY_RATE) / B

    def gram_left(r):
        if r == 0:
            loads[3].wait()
        at_rows = pl.ds(r * COLS, COLS)
        gram = jnp.zeros((COLS, B), F32)
        for s in range(QUARTERS):
            gram += lax.dot_general(
                grads[s, at_rows, :], grads[s], (((1,), (1,)), ((), ())), preferred_element_type=F32
            )
        new_left[at_rows, :] = DECAY_RATE * new_left[at_rows, :] + factor * gram

    def gram_right(r):
        if r == 0:
            loads[4].wait()
        at_rows = pl.ds(r * COLS, COLS)
        turned = grads[r].T
        for s in range(QUARTERS):
            at_cols = pl.ds(s * COLS, COLS)
            gram = jnp.dot(turned, grads[s], preferred_element_type=F32)
            new_right[at_rows, at_cols] = DECAY_RATE * new_right[at_rows, at_cols] + factor * gram

    direction_sum = jnp.zeros((8, LANES), F32)
    for s in range(QUARTERS - 1):
        direction_sum = multiply_right(s, direction_sum)
        back_own(s)
    direction_sum = multiply_right(QUARTERS - 1, direction_sum)
    exchange_start(0, jnp.concatenate([grad_sum, direction_sum], axis=0))
    back_on(0)
    back_own(QUARTERS - 1)
    gram_left(0)
    gram_left(1)
    back_on(1)
    gram_left(2)
    gram_left(3)
    back_on(2)
    for r in range(len(rounds)):
        totals = exchange_end(r)
        if r + 1 < len(rounds):
            exchange_start(r + 1, totals)
        if r < 3:
            gram_right(r)
    for r in range(min(len(rounds), 3), 4):
        gram_right(r)
    grad_total = jnp.sum(totals[0:8], keepdims=True)
    direction_total = jnp.sum(totals[8:16], keepdims=True)
    scale[...] = jnp.broadcast_to(jnp.sqrt(grad_total / (direction_total + EPSILON)), (8, LANES))
    finish(0)
    back_on(3)
    finish(1)
    finish(2)
    finish(3)

    for s in range(QUARTERS):
        all_sent(*there, s)
        all_sent(*back, s)
    for r in range(len(rounds)):
        exchange_sent(r)


def store(wide, scale, left, right, update, new_left, new_right, narrow, sem):
    copies = [
        pltpu.make_async_copy(left, new_left, sem.at[0]),
        pltpu.make_async_copy(right, new_right, sem.at[1]),
    ]
    for copy in copies:
        copy.start()
    rows = PIECE * SUBROWS
    for k in range(HELD):
        part = pl.ds(k * rows, rows)
        narrow[part, :] = (scale[0:1, :] * wide[part, :]).astype(BF16)
        copies.append(pltpu.make_async_copy(narrow.at[part], update.at[part], sem.at[2 + k]))
        copies[-1].start()
    for copy in copies:
        copy.wait()


def local(sizes, gradient, block_position, block_owner, left_stats, right_stats, left_root, right_root):
    xs, ys, zs, cores = sizes
    rounds = sum(size > 1 for size in sizes)
    held_rows = HELD * PIECE * SUBROWS
    outside = pl.BlockSpec(memory_space=pltpu.HBM)
    inside = pl.BlockSpec(memory_space=pltpu.VMEM)

    def quarters(*lead):
        return [pltpu.VMEM((*lead, PIECE, COLS), BF16)] * QUARTERS

    dma = pltpu.SemaphoreType.DMA
    results = pl.pallas_call(
        functools.partial(kernel, sizes),
        out_shape=(
            pltpu.VMEM((held_rows, LANES), F32),
            pltpu.VMEM((8, LANES), F32),
            pltpu.VMEM((B, B), F32),
            pltpu.VMEM((B, B), F32),
        ),
        in_specs=[outside] * 8,
        out_specs=(inside,) * 4,
        scratch_shapes=[
            pltpu.SMEM(block_position.shape, jnp.int32),
            pltpu.SMEM(block_owner.shape, jnp.int32),
            pltpu.SMEM((RING**GROUP_BLOCKS * RING * WORDS,), jnp.int32),
            pltpu.VMEM((held_rows, LANES), BF16),
            pltpu.VMEM((QUARTERS, B, COLS), BF16),
            pltpu.VMEM((B, B), BF16),
            pltpu.VMEM((B, B), BF16),
            pltpu.VMEM((B, B), BF16),
            pltpu.VMEM((B, COLS), F32),
            quarters(HELD),
            quarters(2 * SLOTS),
            quarters(2 * SLOTS),
            quarters(OWNED),
            quarters(2 * SLOTS),
            quarters(2 * SLOTS),
            pltpu.VMEM((rounds, 16, LANES), F32),
            pltpu.VMEM((rounds, 4, 16, LANES), F32),
            dma((8,)),
            dma((QUARTERS,)),
            dma((QUARTERS, 4)),
            dma((QUARTERS,)),
            dma((QUARTERS, 4)),
            dma((rounds,)),
            dma((rounds,)),
        ],
        compiler_params=pltpu.CompilerParams(
            collective_id=0, has_side_effects=True, vmem_limit_bytes=32 * 1024 * 1024
        ),
        name="shampoo",
    )(
        *(
            pltpu.with_memory_space_constraint(value, pltpu.HBM)
            for value in (
                block_position,
                block_owner,
                jnp.asarray(tables()),
                gradient.reshape(held_rows, LANES),
                left_stats[0],
                right_stats[0],
                left_root[0],
                right_root[0],
            )
        )
    )
    update, new_left, new_right = pl.pallas_call(
        store,
        out_shape=(
            jax.ShapeDtypeStruct((held_rows, LANES), BF16),
            jax.ShapeDtypeStruct((B, B), F32),
            jax.ShapeDtypeStruct((B, B), F32),
        ),
        in_specs=[inside] * 4,
        out_specs=(outside,) * 3,
        scratch_shapes=[pltpu.VMEM((held_rows, LANES), BF16), dma((2 + HELD,))],
        compiler_params=pltpu.CompilerParams(vmem_limit_bytes=4 * 1024 * 1024),
        name="store",
    )(*(pltpu.with_memory_space_constraint(value, pltpu.VMEM) for value in results))
    return (update.reshape(-1), new_left[None], new_right[None])


def solution(mesh):
    cores = 2
    sizes = (mesh.shape["mp"] // RING, RING, mesh.shape["dp"] // cores, cores)
    split = P(("dp", "mp"))
    slots = P(("dp", "mp"), None, None)
    return jax.shard_map(
        functools.partial(local, sizes),
        mesh=mesh,
        in_specs=(split, P(), P(), slots, slots, slots, slots),
        out_specs=(split, slots, slots),
        check_vma=False,
    )
```

```python
import functools
import itertools

import jax
import jax.numpy as jnp
import numpy as np
from jax import lax
from jax.experimental import pallas as pl
from jax.experimental.pallas import tpu as pltpu
from jax.sharding import PartitionSpec as P

DECAY_RATE = 0.95
EPSILON = 1e-06
MESH = pl.DeviceIdType.MESH

RING = 4
GROUP_BLOCKS = 3
B = 1024
PIECE = 128
HELD = 6
OWNED = B // PIECE
COLS = 256
QUARTERS = B // COLS
SLOTS = 6
EARLY = 3
EARLIER = B - COLS
WORDS = 8
LANES = 128
SUBROWS = B // LANES
F32, BF16 = jnp.float32, jnp.bfloat16


def schedule(wanted):
    ways = (1, RING - 1)
    far = [i for i in range(RING) if wanted[i][(i + 2) % RING]]
    best = None
    for split in itertools.product(*[range(len(wanted[i][(i + 2) % RING]) + 1) for i in far]):
        plus = dict(zip(far, split))
        first = {}
        for i in range(RING):
            pieces = wanted[i][(i + 2) % RING]
            n = plus.get(i, 0)
            first[i, 0], first[i, 1] = pieces[:n], pieces[n:]
        if max(len(p) for p in first.values()) > EARLY:
            continue
        loads = [
            len(first[i, w]) + len(first[(i - way) % RING, w]) + len(wanted[i][(i + way) % RING])
            for i in range(RING)
            for w, way in enumerate(ways)
        ]
        key = (max(loads), sum(v * v for v in loads))
        if best is None or key < best[0]:
            best = (key, first)
    assert best is not None and best[0][0] <= SLOTS
    first = best[1]
    sent = {}
    for i in range(RING):
        for w, way in enumerate(ways):
            slots = [None] * SLOTS
            for k, piece in enumerate(first[i, w]):
                slots[k] = ("own", piece)
            for k, piece in enumerate(first[(i - way) % RING, w]):
                slots[EARLY + k] = ("pass", piece)
            free = [t for t in range(SLOTS) if slots[t] is None]
            for t, piece in zip(free, wanted[i][(i + way) % RING]):
                slots[t] = ("own", piece)
            sent[i, w] = slots
    return sent


def packed(codes):
    return sum(int(c) << (5 * k) for k, c in enumerate(codes))


def tables():
    out = np.zeros((RING**GROUP_BLOCKS, RING, WORDS), np.int32)
    for owners in itertools.permutations(range(RING), GROUP_BLOCKS):
        row = (owners[0] * RING + owners[1]) * RING + owners[2]
        there = [[[] for _ in range(RING)] for _ in range(RING)]
        back = [[[] for _ in range(RING)] for _ in range(RING)]
        for piece in range(RING * HELD):
            holder, owner = piece // HELD, owners[piece // OWNED]
            there[holder][owner].append(piece)
            back[owner][holder].append(piece)
        for wanted, size, word in ((there, HELD, 0), (back, OWNED, 4)):
            sent = schedule(wanted)
            for i in range(RING):
                for w in range(2):
                    codes = []
                    for entry in sent[i, w]:
                        if entry is None:
                            codes.append(0)
                        elif entry[0] == "own":
                            codes.append(entry[1] % size)
                        else:
                            codes.append(size)
                    out[row, i, word + w] = packed(codes)
                arrived = {}
                for w, way in enumerate((1, RING - 1)):
                    for t, entry in enumerate(sent[(i - way) % RING, w]):
                        if entry is not None:
                            arrived[entry[1]] = size + w * SLOTS + t
                if word == 0:
                    codes = [HELD + 2 * SLOTS] * OWNED
                    if i in owners:
                        first = owners.index(i) * OWNED
                        for q in range(OWNED):
                            piece = first + q
                            mine = piece // HELD == i
                            codes[q] = piece % HELD if mine else arrived[piece]
                    out[row, i, 2] = packed(codes[:6])
                    out[row, i, 3] = packed(codes[6:])
                else:
                    codes = []
                    for k in range(HELD):
                        piece = i * HELD + k
                        mine = owners[piece // OWNED] == i
                        codes.append(piece % OWNED if mine else arrived[piece])
                    out[row, i, 6] = packed(codes)
    return out.reshape(-1)


def code(word, k):
    return lax.bitwise_and(lax.shift_right_logical(word, jnp.int32(5 * k)), jnp.int32(31))


def kernel(
    sizes,
    position_in,
    owner_in,
    table_in,
    gradient,
    left_stats,
    right_stats,
    left_root,
    right_root,
    wide,
    scale,
    new_left,
    new_right,
    position,
    owner,
    table,
    flat,
    grads,
    left,
    right,
    half,
    begun,
    own,
    there_out,
    there_in,
    product,
    back_out,
    back_in,
    sums_out,
    sums_in,
    local_sem,
    there_send,
    there_recv,
    back_send,
    back_recv,
    sums_send,
    sums_recv,
):
    xs, ys, zs, cores = sizes
    dp, mp = lax.axis_index("dp"), lax.axis_index("mp")
    z, core = dp // cores, dp % cores
    x, y = mp // ys, mp % ys

    def at(x, y, z, core):
        return (z * cores + core, x * ys + y)

    neighbours = (at(x, (y + 1) % ys, z, core), at(x, (y + ys - 1) % ys, z, core))

    here = (x, y, z, core)
    rounds = [(place, size) for place, size in ((1, ys), (3, cores), (0, xs), (2, zs)) if size > 1]

    def along(place, size, distance):
        there = list(here)
        there[place] = (here[place] + distance) % size
        return at(*there)

    greeted = [along(place, size, d) for place, size in rounds for d in range(1, size)]

    loads = [
        pltpu.make_async_copy(source, target, local_sem.at[k])
        for k, (source, target) in enumerate(
            (
                (gradient, flat),
                (left_root, left),
                (right_root, right),
                (left_stats, new_left),
                (right_stats, new_right),
                (position_in, position),
                (owner_in, owner),
                (table_in, table),
            )
        )
    ]
    for k in (5, 6, 7, 0, 1, 2, 3, 4):
        loads[k].start()

    barrier = pltpu.get_barrier_semaphore()
    for device in greeted:
        pl.semaphore_signal(barrier, inc=1, device_id=device, device_id_type=MESH)

    group = (dp * (xs * ys) + mp) // RING

    def find(b, found):
        place, device = position[b], owner[b]
        return tuple(
            jnp.where(place == GROUP_BLOCKS * group + k, device, f) for k, f in enumerate(found)
        )

    for k in (5, 6, 7):
        loads[k].wait()
    zero = jnp.int32(0)
    found = lax.fori_loop(0, position.shape[0], find, (zero,) * GROUP_BLOCKS)
    row = zero
    for f in found:
        row = row * RING + (f - RING * group)
    row = jnp.clip(row, 0, RING**GROUP_BLOCKS - 1)
    base = (row * RING + y) * WORDS
    words = [table[base + k] for k in range(7)]

    loads[0].wait()
    grad_sum = jnp.zeros((8, LANES), F32)
    rows = PIECE * SUBROWS
    for k in range(HELD):
        values = flat[pl.ds(k * rows, rows), :].astype(F32)
        wide[pl.ds(k * rows, rows), :] = values
        grad_sum += jnp.sum(jnp.square(values).reshape(rows // 8, 8, LANES), axis=0)

    def take(s):
        for k in range(HELD):
            for h in range(COLS // LANES):
                start = k * rows + s * (COLS // LANES) + h
                block = wide[pl.ds(start, PIECE, stride=SUBROWS), :]
                own[s][k, :, h * LANES : (h + 1) * LANES] = block.astype(BF16)

    def copy_of(out, into, send, recv, s, w, late):
        slots = pl.ds(w * SLOTS + late * EARLY, EARLY)
        return pltpu.make_async_remote_copy(
            src_ref=out[s].at[slots],
            dst_ref=into[s].at[slots],
            send_sem=send.at[s],
            recv_sem=recv.at[s, 2 * late + w],
            device_id=neighbours[w],
            device_id_type=MESH,
        )

    def send_own(out, into, send, recv, source, pair, size, s):
        for w in range(2):
            for t in range(EARLY):
                out[s][w * SLOTS + t] = source[s][jnp.minimum(code(pair[w], t), size - 1)]
            copy_of(out, into, send, recv, s, w, 0).start()

    def send_on(out, into, send, recv, source, pair, size, s):
        for w in range(2):
            copy_of(out, into, send, recv, s, w, 0).wait_recv()
            for t in range(EARLY, SLOTS):
                c = code(pair[w], t)
                passed = into[s][w * SLOTS + t - EARLY]
                mine = source[s][jnp.minimum(c, size - 1)]
                out[s][w * SLOTS + t] = jnp.where(c == size, passed, mine)
            copy_of(out, into, send, recv, s, w, 1).start()

    def arrive(out, into, send, recv, s):
        for w in range(2):
            copy_of(out, into, send, recv, s, w, 1).wait_recv()

    def all_sent(out, into, send, recv, s):
        pltpu.make_async_remote_copy(
            src_ref=out[s],
            dst_ref=into[s],
            send_sem=send.at[s],
            recv_sem=recv.at[s, 0],
            device_id=neighbours[0],
            device_id_type=MESH,
        ).wait_send()

    def pick(source, into, c, size, s):
        mine = source[s][jnp.minimum(c, size - 1)]
        came = into[s][jnp.clip(c - size, 0, 2 * SLOTS - 1)]
        return jnp.where(c < size, mine, came)

    there = (there_out, there_in, there_send, there_recv)
    back = (back_out, back_in, back_send, back_recv)

    def there_own(s):
        take(s)
        send_own(*there, own, words[0:2], HELD, s)

    def there_on(s):
        send_on(*there, own, words[0:2], HELD, s)

    def multiply_left(s):
        arrive(*there, s)
        for q in range(OWNED):
            c = code(words[2 + q // 6], q % 6)
            value = pick(own, there_in, c, HELD, s)
            value = jnp.where(c < HELD + 2 * SLOTS, value, jnp.zeros_like(value))
            grads[s, pl.ds(q * PIECE, PIECE), :] = value
        if s == 0:
            loads[1].wait()

        def tile(r, carry):
            at_rows = pl.ds(pl.multiple_of(r * COLS, COLS), COLS)
            part = jnp.dot(left[at_rows, :], grads[s], preferred_element_type=F32)
            half[at_rows, s * COLS : (s + 1) * COLS] = part.astype(BF16)
            return carry

        lax.fori_loop(0, B // COLS, tile, 0, unroll=True)

    def begin_right():
        loads[2].wait()

        def tile(r, carry):
            at_rows = pl.ds(pl.multiple_of(r * COLS, COLS), COLS)
            begun[at_rows, :] = jnp.dot(
                half[at_rows, :EARLIER], right[:EARLIER, :COLS], preferred_element_type=F32
            )
            return carry

        lax.fori_loop(0, B // COLS, tile, 0, unroll=True)

    pl.semaphore_wait(barrier, len(greeted))
    there_own(0)
    there_own(1)
    there_own(2)
    there_on(0)
    there_own(3)
    there_on(1)
    multiply_left(0)
    there_on(2)
    multiply_left(1)
    there_on(3)
    multiply_left(2)
    begin_right()
    multiply_left(3)

    def multiply_right(s, total):
        def tile(r, total):
            at_rows = pl.ds(pl.multiple_of(r * COLS, COLS), COLS)
            at_cols = pl.ds(s * COLS, COLS)
            if s == 0:
                part = jnp.dot(
                    half[at_rows, EARLIER:], right[EARLIER:, at_cols], preferred_element_type=F32
                )
                part = (begun[at_rows, :] + part).astype(BF16)
            else:
                part = jnp.dot(
                    half[at_rows, :], right[:, at_cols], preferred_element_type=F32
                ).astype(BF16)
            product[s][pl.ds(r * 2, 2)] = part.reshape(2, PIECE, COLS)
            squares = jnp.square(part.astype(F32))
            squares = squares[:, :LANES] + squares[:, LANES:]
            return total + jnp.sum(squares.reshape(COLS // 8, 8, LANES), axis=0)

        return lax.fori_loop(0, B // COLS, tile, total, unroll=True)

    def back_own(s):
        send_own(*back, product, words[4:6], OWNED, s)

    def back_on(s):
        send_on(*back, product, words[4:6], OWNED, s)

    def finish(s):
        arrive(*back, s)
        for k in range(HELD):
            value = pick(product, back_in, code(words[6], k), OWNED, s).astype(F32)
            for h in range(COLS // LANES):
                start = k * rows + s * (COLS // LANES) + h
                wide[pl.ds(start, PIECE, stride=SUBROWS), :] = value[:, h * LANES : (h + 1) * LANES]

    def exchange(r, d):
        place, size = rounds[r]
        return pltpu.make_async_remote_copy(
            src_ref=sums_out.at[r],
            dst_ref=sums_in.at[r, here[place]],
            send_sem=sums_send.at[r],
            recv_sem=sums_recv.at[r],
            device_id=along(place, size, d),
            device_id_type=MESH,
        )

    def exchange_start(r, sums):
        place, size = rounds[r]
        sums_out[r] = sums
        for d in range(1, size):
            exchange(r, d).start()

    def exchange_all(r):
        size = rounds[r][1]
        return pltpu.make_async_remote_copy(
            src_ref=sums_in.at[r, pl.ds(0, size - 1)],
            dst_ref=sums_in.at[r, pl.ds(0, size - 1)],
            send_sem=sums_send.at[r],
            recv_sem=sums_recv.at[r],
            device_id=along(*rounds[r], 1),
            device_id_type=MESH,
        )

    def exchange_end(r):
        place, size = rounds[r]
        sums_in[r, here[place]] = sums_out[r]
        exchange_all(r).wait_recv()
        return sum((sums_in[r, k] for k in range(1, size)), sums_in[r, 0])

    def exchange_sent(r):
        exchange_all(r).wait_send()

    factor = (1.0 - DECAY_RATE) / B

    def gram_left(r):
        if r == 0:
            loads[3].wait()
        at_rows = pl.ds(r * COLS, COLS)
        gram = jnp.zeros((COLS, B), F32)
        for s in range(QUARTERS):
            gram += lax.dot_general(
                grads[s, at_rows, :], grads[s], (((1,), (1,)), ((), ())), preferred_element_type=F32
            )
        new_left[at_rows, :] = DECAY_RATE * new_left[at_rows, :] + factor * gram

    def gram_right(r):
        if r == 0:
            loads[4].wait()
        at_rows = pl.ds(r * COLS, COLS)
        turned = grads[r].T
        for s in range(QUARTERS):
            at_cols = pl.ds(s * COLS, COLS)
            gram = jnp.dot(turned, grads[s], preferred_element_type=F32)
            new_right[at_rows, at_cols] = DECAY_RATE * new_right[at_rows, at_cols] + factor * gram

    direction_sum = jnp.zeros((8, LANES), F32)
    for s in range(QUARTERS - 1):
        direction_sum = multiply_right(s, direction_sum)
        back_own(s)
    direction_sum = multiply_right(QUARTERS - 1, direction_sum)
    exchange_start(0, jnp.concatenate([grad_sum, direction_sum], axis=0))
    back_on(0)
    back_own(QUARTERS - 1)
    gram_left(0)
    gram_left(1)
    back_on(1)
    gram_left(2)
    gram_left(3)
    back_on(2)
    rights = [functools.partial(gram_right, k) for k in range(4)]
    steps = [
        rights[0:2],
        rights[2:4] + [functools.partial(finish, 0), functools.partial(back_on, 3)],
        [functools.partial(finish, 1)],
    ]
    for r in range(len(rounds)):
        totals = exchange_end(r)
        if r + 1 < len(rounds):
            exchange_start(r + 1, totals)
        if r < len(steps):
            for step in steps[r]:
                step()
    for r in range(len(rounds), len(steps)):
        for step in steps[r]:
            step()
    grad_total = jnp.sum(totals[0:8], keepdims=True)
    direction_total = jnp.sum(totals[8:16], keepdims=True)
    scale[...] = jnp.broadcast_to(jnp.sqrt(grad_total / (direction_total + EPSILON)), (8, LANES))
    finish(2)
    finish(3)

    for s in range(QUARTERS):
        all_sent(*there, s)
        all_sent(*back, s)
    for r in range(len(rounds)):
        exchange_sent(r)


def store(wide, scale, left, right, update, new_left, new_right, narrow, sem):
    copies = [
        pltpu.make_async_copy(left, new_left, sem.at[0]),
        pltpu.make_async_copy(right, new_right, sem.at[1]),
    ]
    for copy in copies:
        copy.start()
    rows = PIECE * SUBROWS
    for k in range(HELD):
        part = pl.ds(k * rows, rows)
        narrow[part, :] = (scale[0:1, :] * wide[part, :]).astype(BF16)
        copies.append(pltpu.make_async_copy(narrow.at[part], update.at[part], sem.at[2 + k]))
        copies[-1].start()
    for copy in copies:
        copy.wait()


def local(sizes, gradient, block_position, block_owner, left_stats, right_stats, left_root, right_root):
    xs, ys, zs, cores = sizes
    rounds = sum(size > 1 for size in sizes)
    held_rows = HELD * PIECE * SUBROWS
    outside = pl.BlockSpec(memory_space=pltpu.HBM)
    inside = pl.BlockSpec(memory_space=pltpu.VMEM)

    def quarters(*lead):
        return [pltpu.VMEM((*lead, PIECE, COLS), BF16)] * QUARTERS

    dma = pltpu.SemaphoreType.DMA
    results = pl.pallas_call(
        functools.partial(kernel, sizes),
        out_shape=(
            pltpu.VMEM((held_rows, LANES), F32),
            pltpu.VMEM((8, LANES), F32),
            pltpu.VMEM((B, B), F32),
            pltpu.VMEM((B, B), F32),
        ),
        in_specs=[outside] * 8,
        out_specs=(inside,) * 4,
        scratch_shapes=[
            pltpu.SMEM(block_position.shape, jnp.int32),
            pltpu.SMEM(block_owner.shape, jnp.int32),
            pltpu.SMEM((RING**GROUP_BLOCKS * RING * WORDS,), jnp.int32),
            pltpu.VMEM((held_rows, LANES), BF16),
            pltpu.VMEM((QUARTERS, B, COLS), BF16),
            pltpu.VMEM((B, B), BF16),
            pltpu.VMEM((B, B), BF16),
            pltpu.VMEM((B, B), BF16),
            pltpu.VMEM((B, COLS), F32),
            quarters(HELD),
            quarters(2 * SLOTS),
            quarters(2 * SLOTS),
            quarters(OWNED),
            quarters(2 * SLOTS),
            quarters(2 * SLOTS),
            pltpu.VMEM((rounds, 16, LANES), F32),
            pltpu.VMEM((rounds, 4, 16, LANES), F32),
            dma((8,)),
            dma((QUARTERS,)),
            dma((QUARTERS, 4)),
            dma((QUARTERS,)),
            dma((QUARTERS, 4)),
            dma((rounds,)),
            dma((rounds,)),
        ],
        compiler_params=pltpu.CompilerParams(
            collective_id=0, has_side_effects=True, vmem_limit_bytes=32 * 1024 * 1024
        ),
        name="shampoo",
    )(
        *(
            pltpu.with_memory_space_constraint(value, pltpu.HBM)
            for value in (
                block_position,
                block_owner,
                jnp.asarray(tables()),
                gradient.reshape(held_rows, LANES),
                left_stats[0],
                right_stats[0],
                left_root[0],
                right_root[0],
            )
        )
    )
    update, new_left, new_right = pl.pallas_call(
        store,
        out_shape=(
            jax.ShapeDtypeStruct((held_rows, LANES), BF16),
            jax.ShapeDtypeStruct((B, B), F32),
            jax.ShapeDtypeStruct((B, B), F32),
        ),
        in_specs=[inside] * 4,
        out_specs=(outside,) * 3,
        scratch_shapes=[pltpu.VMEM((held_rows, LANES), BF16), dma((2 + HELD,))],
        compiler_params=pltpu.CompilerParams(vmem_limit_bytes=4 * 1024 * 1024),
        name="store",
    )(*(pltpu.with_memory_space_constraint(value, pltpu.VMEM) for value in results))
    return (update.reshape(-1), new_left[None], new_right[None])


def solution(mesh):
    cores = 2
    sizes = (mesh.shape["mp"] // RING, RING, mesh.shape["dp"] // cores, cores)
    split = P(("dp", "mp"))
    slots = P(("dp", "mp"), None, None)
    return jax.shard_map(
        functools.partial(local, sizes),
        mesh=mesh,
        in_specs=(split, P(), P(), slots, slots, slots, slots),
        out_specs=(split, slots, slots),
        check_vma=False,
    )
```

```python
import functools
import itertools

import jax
import jax.numpy as jnp
import numpy as np
from jax import lax
from jax.experimental import pallas as pl
from jax.experimental.pallas import tpu as pltpu
from jax.sharding import PartitionSpec as P

DECAY_RATE = 0.95
EPSILON = 1e-06
MESH = pl.DeviceIdType.MESH

RING = 4
GROUP_BLOCKS = 3
B = 1024
PIECE = 128
HELD = 6
OWNED = B // PIECE
COLS = 256
QUARTERS = B // COLS
SLOTS = 6
EARLY = 3
EARLIER = B - COLS
WORDS = 8
LANES = 128
HUB = 1
SUBROWS = B // LANES
F32, BF16 = jnp.float32, jnp.bfloat16


def schedule(wanted):
    ways = (1, RING - 1)
    far = [i for i in range(RING) if wanted[i][(i + 2) % RING]]
    best = None
    for split in itertools.product(*[range(len(wanted[i][(i + 2) % RING]) + 1) for i in far]):
        plus = dict(zip(far, split))
        first = {}
        for i in range(RING):
            pieces = wanted[i][(i + 2) % RING]
            n = plus.get(i, 0)
            first[i, 0], first[i, 1] = pieces[:n], pieces[n:]
        if max(len(p) for p in first.values()) > EARLY:
            continue
        loads = [
            len(first[i, w]) + len(first[(i - way) % RING, w]) + len(wanted[i][(i + way) % RING])
            for i in range(RING)
            for w, way in enumerate(ways)
        ]
        key = (max(loads), sum(v * v for v in loads))
        if best is None or key < best[0]:
            best = (key, first)
    assert best is not None and best[0][0] <= SLOTS
    first = best[1]
    sent = {}
    for i in range(RING):
        for w, way in enumerate(ways):
            slots = [None] * SLOTS
            for k, piece in enumerate(first[i, w]):
                slots[k] = ("own", piece)
            for k, piece in enumerate(first[(i - way) % RING, w]):
                slots[EARLY + k] = ("pass", piece)
            free = [t for t in range(SLOTS) if slots[t] is None]
            for t, piece in zip(free, wanted[i][(i + way) % RING]):
                slots[t] = ("own", piece)
            sent[i, w] = slots
    return sent


def packed(codes):
    return sum(int(c) << (5 * k) for k, c in enumerate(codes))


def tables():
    out = np.zeros((RING**GROUP_BLOCKS, RING, WORDS), np.int32)
    for owners in itertools.permutations(range(RING), GROUP_BLOCKS):
        row = (owners[0] * RING + owners[1]) * RING + owners[2]
        there = [[[] for _ in range(RING)] for _ in range(RING)]
        back = [[[] for _ in range(RING)] for _ in range(RING)]
        for piece in range(RING * HELD):
            holder, owner = piece // HELD, owners[piece // OWNED]
            there[holder][owner].append(piece)
            back[owner][holder].append(piece)
        for wanted, size, word in ((there, HELD, 0), (back, OWNED, 4)):
            sent = schedule(wanted)
            for i in range(RING):
                for w in range(2):
                    codes = []
                    for entry in sent[i, w]:
                        if entry is None:
                            codes.append(0)
                        elif entry[0] == "own":
                            codes.append(entry[1] % size)
                        else:
                            codes.append(size)
                    out[row, i, word + w] = packed(codes)
                arrived = {}
                for w, way in enumerate((1, RING - 1)):
                    for t, entry in enumerate(sent[(i - way) % RING, w]):
                        if entry is not None:
                            arrived[entry[1]] = size + w * SLOTS + t
                if word == 0:
                    codes = [HELD + 2 * SLOTS] * OWNED
                    if i in owners:
                        first = owners.index(i) * OWNED
                        for q in range(OWNED):
                            piece = first + q
                            mine = piece // HELD == i
                            codes[q] = piece % HELD if mine else arrived[piece]
                    out[row, i, 2] = packed(codes[:6])
                    out[row, i, 3] = packed(codes[6:])
                else:
                    codes = []
                    for k in range(HELD):
                        piece = i * HELD + k
                        mine = owners[piece // OWNED] == i
                        codes.append(piece % OWNED if mine else arrived[piece])
                    out[row, i, 6] = packed(codes)
    return out.reshape(-1)


def code(word, k):
    return lax.bitwise_and(lax.shift_right_logical(word, jnp.int32(5 * k)), jnp.int32(31))


def kernel(
    sizes,
    position_in,
    owner_in,
    table_in,
    gradient,
    left_stats,
    right_stats,
    left_root,
    right_root,
    wide,
    scale,
    new_left,
    new_right,
    position,
    owner,
    table,
    flat,
    grads,
    left,
    right,
    half,
    begun,
    own,
    there_out,
    there_in,
    product,
    back_out,
    back_in,
    sums_out,
    sums_in,
    local_sem,
    there_send,
    there_recv,
    back_send,
    back_recv,
    sums_send,
    sums_recv,
):
    xs, ys, zs, cores = sizes
    dp, mp = lax.axis_index("dp"), lax.axis_index("mp")
    z, core = dp // cores, dp % cores
    x, y = mp // ys, mp % ys

    def at(x, y, z, core):
        return (z * cores + core, x * ys + y)

    neighbours = (at(x, (y + 1) % ys, z, core), at(x, (y + ys - 1) % ys, z, core))

    here = (x, y, z, core)
    rounds = [(place, size) for place, size in ((1, ys), (3, cores), (0, xs)) if size > 1]

    def along(place, size, distance):
        there = list(here)
        there[place] = (here[place] + distance) % size
        return at(*there)

    greeted = [along(place, size, d) for place, size in rounds for d in range(1, size)]

    loads = [
        pltpu.make_async_copy(source, target, local_sem.at[k])
        for k, (source, target) in enumerate(
            (
                (gradient, flat),
                (left_root, left),
                (right_root, right),
                (left_stats, new_left),
                (right_stats, new_right),
                (position_in, position),
                (owner_in, owner),
                (table_in, table),
            )
        )
    ]
    for k in (5, 6, 7, 0, 1, 2, 3, 4):
        loads[k].start()

    barrier = pltpu.get_barrier_semaphore()
    for device in greeted:
        pl.semaphore_signal(barrier, inc=1, device_id=device, device_id_type=MESH)
    planes = len(greeted)
    if zs > 1:
        planes += jnp.where(z == HUB, zs - 1, 1)

        @pl.when(z == HUB)
        def _():
            for d in range(1, zs):
                pl.semaphore_signal(barrier, inc=1, device_id=along(2, zs, d), device_id_type=MESH)

        @pl.when(z != HUB)
        def _():
            pl.semaphore_signal(
                barrier, inc=1, device_id=at(x, y, HUB, core), device_id_type=MESH
            )


    group = (dp * (xs * ys) + mp) // RING

    def find(b, found):
        place, device = position[b], owner[b]
        return tuple(
            jnp.where(place == GROUP_BLOCKS * group + k, device, f) for k, f in enumerate(found)
        )

    for k in (5, 6, 7):
        loads[k].wait()
    zero = jnp.int32(0)
    found = lax.fori_loop(0, position.shape[0], find, (zero,) * GROUP_BLOCKS)
    row = zero
    for f in found:
        row = row * RING + (f - RING * group)
    row = jnp.clip(row, 0, RING**GROUP_BLOCKS - 1)
    base = (row * RING + y) * WORDS
    words = [table[base + k] for k in range(7)]

    loads[0].wait()
    grad_sum = jnp.zeros((8, LANES), F32)
    rows = PIECE * SUBROWS
    for k in range(HELD):
        values = flat[pl.ds(k * rows, rows), :].astype(F32)
        wide[pl.ds(k * rows, rows), :] = values
        grad_sum += jnp.sum(jnp.square(values).reshape(rows // 8, 8, LANES), axis=0)

    def take(s):
        for k in range(HELD):
            for h in range(COLS // LANES):
                start = k * rows + s * (COLS // LANES) + h
                block = wide[pl.ds(start, PIECE, stride=SUBROWS), :]
                own[s][k, :, h * LANES : (h + 1) * LANES] = block.astype(BF16)

    def copy_of(out, into, send, recv, s, w, late):
        slots = pl.ds(w * SLOTS + late * EARLY, EARLY)
        return pltpu.make_async_remote_copy(
            src_ref=out[s].at[slots],
            dst_ref=into[s].at[slots],
            send_sem=send.at[s],
            recv_sem=recv.at[s, 2 * late + w],
            device_id=neighbours[w],
            device_id_type=MESH,
        )

    def send_own(out, into, send, recv, source, pair, size, s):
        for w in range(2):
            for t in range(EARLY):
                out[s][w * SLOTS + t] = source[s][jnp.minimum(code(pair[w], t), size - 1)]
            copy_of(out, into, send, recv, s, w, 0).start()

    def send_on(out, into, send, recv, source, pair, size, s):
        for w in range(2):
            copy_of(out, into, send, recv, s, w, 0).wait_recv()
            for t in range(EARLY, SLOTS):
                c = code(pair[w], t)
                passed = into[s][w * SLOTS + t - EARLY]
                mine = source[s][jnp.minimum(c, size - 1)]
                out[s][w * SLOTS + t] = jnp.where(c == size, passed, mine)
            copy_of(out, into, send, recv, s, w, 1).start()

    def arrive(out, into, send, recv, s):
        for w in range(2):
            copy_of(out, into, send, recv, s, w, 1).wait_recv()

    def all_sent(out, into, send, recv, s):
        pltpu.make_async_remote_copy(
            src_ref=out[s],
            dst_ref=into[s],
            send_sem=send.at[s],
            recv_sem=recv.at[s, 0],
            device_id=neighbours[0],
            device_id_type=MESH,
        ).wait_send()

    def pick(source, into, c, size, s):
        mine = source[s][jnp.minimum(c, size - 1)]
        came = into[s][jnp.clip(c - size, 0, 2 * SLOTS - 1)]
        return jnp.where(c < size, mine, came)

    there = (there_out, there_in, there_send, there_recv)
    back = (back_out, back_in, back_send, back_recv)

    def there_own(s):
        take(s)
        send_own(*there, own, words[0:2], HELD, s)

    def there_on(s):
        send_on(*there, own, words[0:2], HELD, s)

    def multiply_left(s):
        arrive(*there, s)
        for q in range(OWNED):
            c = code(words[2 + q // 6], q % 6)
            value = pick(own, there_in, c, HELD, s)
            value = jnp.where(c < HELD + 2 * SLOTS, value, jnp.zeros_like(value))
            grads[s, pl.ds(q * PIECE, PIECE), :] = value
        if s == 0:
            loads[1].wait()

        def tile(r, carry):
            at_rows = pl.ds(pl.multiple_of(r * COLS, COLS), COLS)
            part = jnp.dot(left[at_rows, :], grads[s], preferred_element_type=F32)
            half[at_rows, s * COLS : (s + 1) * COLS] = part.astype(BF16)
            return carry

        lax.fori_loop(0, B // COLS, tile, 0, unroll=True)

    def begin_right():
        loads[2].wait()

        def tile(r, carry):
            at_rows = pl.ds(pl.multiple_of(r * COLS, COLS), COLS)
            begun[at_rows, :] = jnp.dot(
                half[at_rows, :EARLIER], right[:EARLIER, :COLS], preferred_element_type=F32
            )
            return carry

        lax.fori_loop(0, B // COLS, tile, 0, unroll=True)

    pl.semaphore_wait(barrier, planes)
    there_own(0)
    there_own(1)
    there_own(2)
    there_on(0)
    there_own(3)
    there_on(1)
    multiply_left(0)
    there_on(2)
    multiply_left(1)
    there_on(3)
    multiply_left(2)
    begin_right()
    multiply_left(3)

    def multiply_right(s, total):
        def tile(r, total):
            at_rows = pl.ds(pl.multiple_of(r * COLS, COLS), COLS)
            at_cols = pl.ds(s * COLS, COLS)
            if s == 0:
                part = jnp.dot(
                    half[at_rows, EARLIER:], right[EARLIER:, at_cols], preferred_element_type=F32
                )
                part = (begun[at_rows, :] + part).astype(BF16)
            else:
                part = jnp.dot(
                    half[at_rows, :], right[:, at_cols], preferred_element_type=F32
                ).astype(BF16)
            product[s][pl.ds(r * 2, 2)] = part.reshape(2, PIECE, COLS)
            squares = jnp.square(part.astype(F32))
            squares = squares[:, :LANES] + squares[:, LANES:]
            return total + jnp.sum(squares.reshape(COLS // 8, 8, LANES), axis=0)

        return lax.fori_loop(0, B // COLS, tile, total, unroll=True)

    def back_own(s):
        send_own(*back, product, words[4:6], OWNED, s)

    def back_on(s):
        send_on(*back, product, words[4:6], OWNED, s)

    def finish(s):
        arrive(*back, s)
        for k in range(HELD):
            value = pick(product, back_in, code(words[6], k), OWNED, s).astype(F32)
            for h in range(COLS // LANES):
                start = k * rows + s * (COLS // LANES) + h
                wide[pl.ds(start, PIECE, stride=SUBROWS), :] = value[:, h * LANES : (h + 1) * LANES]

    def exchange(r, d):
        place, size = rounds[r]
        return pltpu.make_async_remote_copy(
            src_ref=sums_out.at[r],
            dst_ref=sums_in.at[r, here[place]],
            send_sem=sums_send.at[r],
            recv_sem=sums_recv.at[r],
            device_id=along(place, size, d),
            device_id_type=MESH,
        )

    def exchange_start(r, sums):
        place, size = rounds[r]
        sums_out[r] = sums
        for d in range(1, size):
            exchange(r, d).start()

    def exchange_all(r):
        size = rounds[r][1]
        return pltpu.make_async_remote_copy(
            src_ref=sums_in.at[r, pl.ds(0, size - 1)],
            dst_ref=sums_in.at[r, pl.ds(0, size - 1)],
            send_sem=sums_send.at[r],
            recv_sem=sums_recv.at[r],
            device_id=along(*rounds[r], 1),
            device_id_type=MESH,
        )

    def exchange_end(r):
        place, size = rounds[r]
        sums_in[r, here[place]] = sums_out[r]
        exchange_all(r).wait_recv()
        return sum((sums_in[r, k] for k in range(1, size)), sums_in[r, 0])

    def exchange_sent(r):
        exchange_all(r).wait_send()

    gather, spread = len(rounds), len(rounds) + 1

    def plane_copy(r, source, target, device):
        return pltpu.make_async_remote_copy(
            src_ref=source,
            dst_ref=target,
            send_sem=sums_send.at[r],
            recv_sem=sums_recv.at[r],
            device_id=device,
            device_id_type=MESH,
        )

    def plane_all(r, count):
        part = sums_in.at[r, pl.ds(0, count)]
        return plane_copy(r, part, part, along(2, zs, 1))

    def planes_gather(sums):
        sums_out[gather] = sums

        @pl.when(z != HUB)
        def _():
            to = sums_in.at[gather, z]
            plane_copy(gather, sums_out.at[gather], to, at(x, y, HUB, core)).start()

    def planes_spread():
        @pl.when(z == HUB)
        def _():
            plane_all(gather, zs - 1).wait_recv()
            sums_in[gather, HUB] = sums_out[gather]
            total = sum((sums_in[gather, k] for k in range(1, zs)), sums_in[gather, 0])
            sums_out[spread] = total
            sums_in[spread, 0] = total
            for d in range(1, zs):
                to = sums_in.at[spread, 0]
                plane_copy(spread, sums_out.at[spread], to, along(2, zs, d)).start()

    def planes_end():
        @pl.when(z != HUB)
        def _():
            plane_all(spread, 1).wait_recv()

        return sums_in[spread, 0]

    def planes_sent():
        @pl.when(z == HUB)
        def _():
            plane_all(spread, zs - 1).wait_send()

        @pl.when(z != HUB)
        def _():
            plane_all(gather, 1).wait_send()

    factor = (1.0 - DECAY_RATE) / B

    def gram_left(r):
        if r == 0:
            loads[3].wait()
        at_rows = pl.ds(r * COLS, COLS)
        gram = jnp.zeros((COLS, B), F32)
        for s in range(QUARTERS):
            gram += lax.dot_general(
                grads[s, at_rows, :], grads[s], (((1,), (1,)), ((), ())), preferred_element_type=F32
            )
        new_left[at_rows, :] = DECAY_RATE * new_left[at_rows, :] + factor * gram

    def gram_right(r):
        if r == 0:
            loads[4].wait()
        at_rows = pl.ds(r * COLS, COLS)
        turned = grads[r].T
        for s in range(QUARTERS):
            at_cols = pl.ds(s * COLS, COLS)
            gram = jnp.dot(turned, grads[s], preferred_element_type=F32)
            new_right[at_rows, at_cols] = DECAY_RATE * new_right[at_rows, at_cols] + factor * gram

    direction_sum = jnp.zeros((8, LANES), F32)
    for s in range(QUARTERS - 1):
        direction_sum = multiply_right(s, direction_sum)
        back_own(s)
    direction_sum = multiply_right(QUARTERS - 1, direction_sum)
    exchange_start(0, jnp.concatenate([grad_sum, direction_sum], axis=0))
    back_on(0)
    back_own(QUARTERS - 1)
    gram_left(0)
    gram_left(1)
    back_on(1)
    gram_left(2)
    gram_left(3)
    back_on(2)
    rights = [functools.partial(gram_right, k) for k in range(4)]
    steps = [
        rights[0:2],
        rights[2:4] + [functools.partial(finish, 0), functools.partial(back_on, 3)],
        [],
    ]
    for r in range(len(rounds)):
        totals = exchange_end(r)
        if r + 1 < len(rounds):
            exchange_start(r + 1, totals)
        for step in steps[r]:
            step()
    for r in range(len(rounds), len(steps)):
        for step in steps[r]:
            step()
    if zs > 1:
        planes_gather(totals)
    finish(1)
    if zs > 1:
        planes_spread()
    finish(2)
    if zs > 1:
        totals = planes_end()
    grad_total = jnp.sum(totals[0:8], keepdims=True)
    direction_total = jnp.sum(totals[8:16], keepdims=True)
    scale[...] = jnp.broadcast_to(jnp.sqrt(grad_total / (direction_total + EPSILON)), (8, LANES))
    finish(3)

    for s in range(QUARTERS):
        all_sent(*there, s)
        all_sent(*back, s)
    for r in range(len(rounds)):
        exchange_sent(r)
    if zs > 1:
        planes_sent()


def store(wide, scale, left, right, update, new_left, new_right, narrow, sem):
    copies = [
        pltpu.make_async_copy(left, new_left, sem.at[0]),
        pltpu.make_async_copy(right, new_right, sem.at[1]),
    ]
    for copy in copies:
        copy.start()
    rows = PIECE * SUBROWS
    for k in range(HELD):
        part = pl.ds(k * rows, rows)
        narrow[part, :] = (scale[0:1, :] * wide[part, :]).astype(BF16)
        copies.append(pltpu.make_async_copy(narrow.at[part], update.at[part], sem.at[2 + k]))
        copies[-1].start()
    for copy in copies:
        copy.wait()


def local(sizes, gradient, block_position, block_owner, left_stats, right_stats, left_root, right_root):
    xs, ys, zs, cores = sizes
    rounds = sum(size > 1 for size in sizes) + 1
    held_rows = HELD * PIECE * SUBROWS
    outside = pl.BlockSpec(memory_space=pltpu.HBM)
    inside = pl.BlockSpec(memory_space=pltpu.VMEM)

    def quarters(*lead):
        return [pltpu.VMEM((*lead, PIECE, COLS), BF16)] * QUARTERS

    dma = pltpu.SemaphoreType.DMA
    results = pl.pallas_call(
        functools.partial(kernel, sizes),
        out_shape=(
            pltpu.VMEM((held_rows, LANES), F32),
            pltpu.VMEM((8, LANES), F32),
            pltpu.VMEM((B, B), F32),
            pltpu.VMEM((B, B), F32),
        ),
        in_specs=[outside] * 8,
        out_specs=(inside,) * 4,
        scratch_shapes=[
            pltpu.SMEM(block_position.shape, jnp.int32),
            pltpu.SMEM(block_owner.shape, jnp.int32),
            pltpu.SMEM((RING**GROUP_BLOCKS * RING * WORDS,), jnp.int32),
            pltpu.VMEM((held_rows, LANES), BF16),
            pltpu.VMEM((QUARTERS, B, COLS), BF16),
            pltpu.VMEM((B, B), BF16),
            pltpu.VMEM((B, B), BF16),
            pltpu.VMEM((B, B), BF16),
            pltpu.VMEM((B, COLS), F32),
            quarters(HELD),
            quarters(2 * SLOTS),
            quarters(2 * SLOTS),
            quarters(OWNED),
            quarters(2 * SLOTS),
            quarters(2 * SLOTS),
            pltpu.VMEM((rounds, 16, LANES), F32),
            pltpu.VMEM((rounds, 4, 16, LANES), F32),
            dma((8,)),
            dma((QUARTERS,)),
            dma((QUARTERS, 4)),
            dma((QUARTERS,)),
            dma((QUARTERS, 4)),
            dma((rounds,)),
            dma((rounds,)),
        ],
        compiler_params=pltpu.CompilerParams(
            collective_id=0, has_side_effects=True, vmem_limit_bytes=32 * 1024 * 1024
        ),
        name="shampoo",
    )(
        *(
            pltpu.with_memory_space_constraint(value, pltpu.HBM)
            for value in (
                block_position,
                block_owner,
                jnp.asarray(tables()),
                gradient.reshape(held_rows, LANES),
                left_stats[0],
                right_stats[0],
                left_root[0],
                right_root[0],
            )
        )
    )
    update, new_left, new_right = pl.pallas_call(
        store,
        out_shape=(
            jax.ShapeDtypeStruct((held_rows, LANES), BF16),
            jax.ShapeDtypeStruct((B, B), F32),
            jax.ShapeDtypeStruct((B, B), F32),
        ),
        in_specs=[inside] * 4,
        out_specs=(outside,) * 3,
        scratch_shapes=[pltpu.VMEM((held_rows, LANES), BF16), dma((2 + HELD,))],
        compiler_params=pltpu.CompilerParams(vmem_limit_bytes=4 * 1024 * 1024),
        name="store",
    )(*(pltpu.with_memory_space_constraint(value, pltpu.VMEM) for value in results))
    return (update.reshape(-1), new_left[None], new_right[None])


def solution(mesh):
    cores = 2
    sizes = (mesh.shape["mp"] // RING, RING, mesh.shape["dp"] // cores, cores)
    split = P(("dp", "mp"))
    slots = P(("dp", "mp"), None, None)
    return jax.shard_map(
        functools.partial(local, sizes),
        mesh=mesh,
        in_specs=(split, P(), P(), slots, slots, slots, slots),
        out_specs=(split, slots, slots),
        check_vma=False,
    )
```

```python
import functools
import itertools

import jax
import jax.numpy as jnp
import numpy as np
from jax import lax
from jax.experimental import pallas as pl
from jax.experimental.pallas import tpu as pltpu
from jax.sharding import PartitionSpec as P

DECAY_RATE = 0.95
EPSILON = 1e-06
MESH = pl.DeviceIdType.MESH

RING = 4
GROUP_BLOCKS = 3
B = 1024
PIECE = 128
HELD = 6
OWNED = B // PIECE
COLS = 256
QUARTERS = B // COLS
SLOTS = 6
EARLY = 3
EARLIER = B - COLS
WORDS = 8
LANES = 128
HUB = 1
SUBROWS = B // LANES
F32, BF16 = jnp.float32, jnp.bfloat16


def schedule(wanted):
    ways = (1, RING - 1)
    far = [i for i in range(RING) if wanted[i][(i + 2) % RING]]
    best = None
    for split in itertools.product(*[range(len(wanted[i][(i + 2) % RING]) + 1) for i in far]):
        plus = dict(zip(far, split))
        first = {}
        for i in range(RING):
            pieces = wanted[i][(i + 2) % RING]
            n = plus.get(i, 0)
            first[i, 0], first[i, 1] = pieces[:n], pieces[n:]
        if max(len(p) for p in first.values()) > EARLY:
            continue
        loads = [
            len(first[i, w]) + len(first[(i - way) % RING, w]) + len(wanted[i][(i + way) % RING])
            for i in range(RING)
            for w, way in enumerate(ways)
        ]
        key = (max(loads), sum(v * v for v in loads))
        if best is None or key < best[0]:
            best = (key, first)
    assert best is not None and best[0][0] <= SLOTS
    first = best[1]
    sent = {}
    for i in range(RING):
        for w, way in enumerate(ways):
            slots = [None] * SLOTS
            for k, piece in enumerate(first[i, w]):
                slots[k] = ("own", piece)
            for k, piece in enumerate(first[(i - way) % RING, w]):
                slots[EARLY + k] = ("pass", piece)
            free = [t for t in range(SLOTS) if slots[t] is None]
            for t, piece in zip(free, wanted[i][(i + way) % RING]):
                slots[t] = ("own", piece)
            sent[i, w] = slots
    return sent


def packed(codes):
    return sum(int(c) << (5 * k) for k, c in enumerate(codes))


def tables():
    out = np.zeros((RING**GROUP_BLOCKS, RING, WORDS), np.int32)
    for owners in itertools.permutations(range(RING), GROUP_BLOCKS):
        row = (owners[0] * RING + owners[1]) * RING + owners[2]
        there = [[[] for _ in range(RING)] for _ in range(RING)]
        back = [[[] for _ in range(RING)] for _ in range(RING)]
        for piece in range(RING * HELD):
            holder, owner = piece // HELD, owners[piece // OWNED]
            there[holder][owner].append(piece)
            back[owner][holder].append(piece)
        for wanted, size, word in ((there, HELD, 0), (back, OWNED, 4)):
            sent = schedule(wanted)
            for i in range(RING):
                for w in range(2):
                    codes = []
                    for entry in sent[i, w]:
                        if entry is None:
                            codes.append(0)
                        elif entry[0] == "own":
                            codes.append(entry[1] % size)
                        else:
                            codes.append(size)
                    out[row, i, word + w] = packed(codes)
                arrived = {}
                for w, way in enumerate((1, RING - 1)):
                    for t, entry in enumerate(sent[(i - way) % RING, w]):
                        if entry is not None:
                            arrived[entry[1]] = size + w * SLOTS + t
                if word == 0:
                    codes = [HELD + 2 * SLOTS] * OWNED
                    if i in owners:
                        first = owners.index(i) * OWNED
                        for q in range(OWNED):
                            piece = first + q
                            mine = piece // HELD == i
                            codes[q] = piece % HELD if mine else arrived[piece]
                    out[row, i, 2] = packed(codes[:6])
                    out[row, i, 3] = packed(codes[6:])
                else:
                    codes = []
                    for k in range(HELD):
                        piece = i * HELD + k
                        mine = owners[piece // OWNED] == i
                        codes.append(piece % OWNED if mine else arrived[piece])
                    out[row, i, 6] = packed(codes)
    return out.reshape(-1)


def code(word, k):
    return lax.bitwise_and(lax.shift_right_logical(word, jnp.int32(5 * k)), jnp.int32(31))


def kernel(
    sizes,
    position_in,
    owner_in,
    table_in,
    gradient,
    left_stats,
    right_stats,
    left_root,
    right_root,
    wide,
    scale,
    new_left,
    new_right,
    position,
    owner,
    table,
    flat,
    grads,
    left,
    right,
    half,
    begun,
    own,
    there_out,
    there_in,
    product,
    back_out,
    back_in,
    sums_out,
    sums_in,
    local_sem,
    there_send,
    there_recv,
    back_send,
    back_recv,
    sums_send,
    sums_recv,
):
    xs, ys, zs, cores = sizes
    dp, mp = lax.axis_index("dp"), lax.axis_index("mp")
    z, core = dp // cores, dp % cores
    x, y = mp // ys, mp % ys

    def at(x, y, z, core):
        return (z * cores + core, x * ys + y)

    neighbours = (at(x, (y + 1) % ys, z, core), at(x, (y + ys - 1) % ys, z, core))

    here = (x, y, z, core)
    rounds = [(place, size) for place, size in ((1, ys), (3, cores), (0, xs)) if size > 1]

    def along(place, size, distance):
        there = list(here)
        there[place] = (here[place] + distance) % size
        return at(*there)

    greeted = [along(place, size, d) for place, size in rounds for d in range(1, size)]

    rows = PIECE * SUBROWS
    parts = [pl.ds(k * rows, rows) for k in range(HELD)]
    loads = [
        pltpu.make_async_copy(source, target, local_sem.at[k])
        for k, (source, target) in enumerate(
            (
                (left_root, left),
                (right_root, right),
                (left_stats, new_left),
                (right_stats, new_right),
                (position_in, position),
                (owner_in, owner),
                (table_in, table),
                *((gradient.at[part], flat.at[part]) for part in parts),
            )
        )
    ]
    for k in (4, 5, 6, *range(7, 7 + HELD), 0, 1, 2, 3):
        loads[k].start()

    barrier = pltpu.get_barrier_semaphore()
    for device in greeted:
        pl.semaphore_signal(barrier, inc=1, device_id=device, device_id_type=MESH)
    planes = len(greeted)
    if zs > 1:
        planes += jnp.where(z == HUB, zs - 1, 1)

        @pl.when(z == HUB)
        def _():
            for d in range(1, zs):
                pl.semaphore_signal(barrier, inc=1, device_id=along(2, zs, d), device_id_type=MESH)

        @pl.when(z != HUB)
        def _():
            pl.semaphore_signal(
                barrier, inc=1, device_id=at(x, y, HUB, core), device_id_type=MESH
            )


    group = (dp * (xs * ys) + mp) // RING

    def find(b, found):
        place, device = position[b], owner[b]
        return tuple(
            jnp.where(place == GROUP_BLOCKS * group + k, device, f) for k, f in enumerate(found)
        )

    for k in (4, 5, 6):
        loads[k].wait()
    zero = jnp.int32(0)
    found = lax.fori_loop(0, position.shape[0], find, (zero,) * GROUP_BLOCKS)
    row = zero
    for f in found:
        row = row * RING + (f - RING * group)
    row = jnp.clip(row, 0, RING**GROUP_BLOCKS - 1)
    base = (row * RING + y) * WORDS
    words = [table[base + k] for k in range(7)]

    for k, part in enumerate(parts):
        loads[7 + k].wait()
        wide[part, :] = flat[part, :].astype(F32)

    def take(s):
        for k in range(HELD):
            for h in range(COLS // LANES):
                start = k * rows + s * (COLS // LANES) + h
                block = wide[pl.ds(start, PIECE, stride=SUBROWS), :]
                own[s][k, :, h * LANES : (h + 1) * LANES] = block.astype(BF16)

    def copy_of(out, into, send, recv, s, w, late):
        slots = pl.ds(w * SLOTS + late * EARLY, EARLY)
        return pltpu.make_async_remote_copy(
            src_ref=out[s].at[slots],
            dst_ref=into[s].at[slots],
            send_sem=send.at[s],
            recv_sem=recv.at[s, 2 * late + w],
            device_id=neighbours[w],
            device_id_type=MESH,
        )

    def send_own(out, into, send, recv, source, pair, size, s):
        for w in range(2):
            for t in range(EARLY):
                out[s][w * SLOTS + t] = source[s][jnp.minimum(code(pair[w], t), size - 1)]
            copy_of(out, into, send, recv, s, w, 0).start()

    def send_on(out, into, send, recv, source, pair, size, s):
        for w in range(2):
            copy_of(out, into, send, recv, s, w, 0).wait_recv()
            for t in range(EARLY, SLOTS):
                c = code(pair[w], t)
                passed = into[s][w * SLOTS + t - EARLY]
                mine = source[s][jnp.minimum(c, size - 1)]
                out[s][w * SLOTS + t] = jnp.where(c == size, passed, mine)
            copy_of(out, into, send, recv, s, w, 1).start()

    def arrive(out, into, send, recv, s):
        for w in range(2):
            copy_of(out, into, send, recv, s, w, 1).wait_recv()

    def all_sent(out, into, send, recv, s):
        pltpu.make_async_remote_copy(
            src_ref=out[s],
            dst_ref=into[s],
            send_sem=send.at[s],
            recv_sem=recv.at[s, 0],
            device_id=neighbours[0],
            device_id_type=MESH,
        ).wait_send()

    def pick(source, into, c, size, s):
        mine = source[s][jnp.minimum(c, size - 1)]
        came = into[s][jnp.clip(c - size, 0, 2 * SLOTS - 1)]
        return jnp.where(c < size, mine, came)

    there = (there_out, there_in, there_send, there_recv)
    back = (back_out, back_in, back_send, back_recv)

    def there_own(s):
        take(s)
        send_own(*there, own, words[0:2], HELD, s)

    def there_on(s):
        send_on(*there, own, words[0:2], HELD, s)

    def assemble(s):
        arrive(*there, s)
        for q in range(OWNED):
            c = code(words[2 + q // 6], q % 6)
            value = pick(own, there_in, c, HELD, s)
            value = jnp.where(c < HELD + 2 * SLOTS, value, jnp.zeros_like(value))
            grads[s, pl.ds(q * PIECE, PIECE), :] = value

    def multiply_left(s):
        if s == 0:
            loads[0].wait()

        def tile(r, carry):
            at_rows = pl.ds(pl.multiple_of(r * COLS, COLS), COLS)
            roots = left[pl.ds(r * 2, 2)].reshape(COLS, B)
            part = jnp.dot(roots, grads[s], preferred_element_type=F32)
            half[at_rows, s * COLS : (s + 1) * COLS] = part.astype(BF16)
            return carry

        lax.fori_loop(0, B // COLS, tile, 0, unroll=True)

    def begin_right():
        loads[1].wait()

        def tile(r, carry):
            at_rows = pl.ds(pl.multiple_of(r * COLS, COLS), COLS)
            part = jnp.dot(
                half[at_rows, :EARLIER], right[:EARLIER, :COLS], preferred_element_type=F32
            )
            begun[pl.ds(r * 2, 2)] = part.reshape(2, PIECE, COLS)
            return carry

        lax.fori_loop(0, B // COLS, tile, 0, unroll=True)

    def back_first():
        last = QUARTERS - 1
        for t in range(EARLY):
            places = [jnp.minimum(code(words[4 + w], t), OWNED - 1) for w in range(2)]
            roots = jnp.concatenate([left[q] for q in places], axis=0)
            start = jnp.concatenate([begun[q] for q in places], axis=0)
            part = jnp.dot(roots, grads[last], preferred_element_type=F32).astype(BF16)
            part = jnp.dot(part, right[EARLIER:, :COLS], preferred_element_type=F32)
            part = (start + part).astype(BF16)
            for w in range(2):
                slot = w * SLOTS + t
                back_out[0][slot] = part[w * PIECE : (w + 1) * PIECE]
                pltpu.make_async_remote_copy(
                    src_ref=back_out[0].at[slot],
                    dst_ref=back_in[0].at[slot],
                    send_sem=back_send.at[0],
                    recv_sem=back_recv.at[0, w],
                    device_id=neighbours[w],
                    device_id_type=MESH,
                ).start()

    pl.semaphore_wait(barrier, planes)
    there_own(0)
    there_own(1)
    there_own(2)
    grad_sum = jnp.zeros((8, LANES), F32)
    for part in parts:
        squares = jnp.square(wide[part, :])
        grad_sum += jnp.sum(squares.reshape(rows // 8, 8, LANES), axis=0)
    there_on(0)
    there_own(3)
    there_on(1)
    assemble(0)
    multiply_left(0)
    there_on(2)
    assemble(1)
    multiply_left(1)
    there_on(3)
    assemble(2)
    multiply_left(2)
    begin_right()
    assemble(3)
    back_first()
    multiply_left(3)

    def multiply_right(s, total):
        def tile(r, total):
            at_rows = pl.ds(pl.multiple_of(r * COLS, COLS), COLS)
            at_cols = pl.ds(s * COLS, COLS)
            if s == 0:
                part = jnp.dot(
                    half[at_rows, EARLIER:], right[EARLIER:, at_cols], preferred_element_type=F32
                )
                part = (begun[pl.ds(r * 2, 2)].reshape(COLS, COLS) + part).astype(BF16)
            else:
                part = jnp.dot(
                    half[at_rows, :], right[:, at_cols], preferred_element_type=F32
                ).astype(BF16)
            product[s][pl.ds(r * 2, 2)] = part.reshape(2, PIECE, COLS)
            squares = jnp.square(part.astype(F32))
            squares = squares[:, :LANES] + squares[:, LANES:]
            return total + jnp.sum(squares.reshape(COLS // 8, 8, LANES), axis=0)

        return lax.fori_loop(0, B // COLS, tile, total, unroll=True)

    def back_own(s):
        send_own(*back, product, words[4:6], OWNED, s)

    def back_on(s):
        send_on(*back, product, words[4:6], OWNED, s)

    def finish(s):
        arrive(*back, s)
        for k in range(HELD):
            value = pick(product, back_in, code(words[6], k), OWNED, s).astype(F32)
            for h in range(COLS // LANES):
                start = k * rows + s * (COLS // LANES) + h
                wide[pl.ds(start, PIECE, stride=SUBROWS), :] = value[:, h * LANES : (h + 1) * LANES]

    def exchange(r, d):
        place, size = rounds[r]
        return pltpu.make_async_remote_copy(
            src_ref=sums_out.at[r],
            dst_ref=sums_in.at[r, here[place]],
            send_sem=sums_send.at[r],
            recv_sem=sums_recv.at[r],
            device_id=along(place, size, d),
            device_id_type=MESH,
        )

    def exchange_start(r, sums):
        place, size = rounds[r]
        sums_out[r] = sums
        for d in range(1, size):
            exchange(r, d).start()

    def exchange_all(r):
        size = rounds[r][1]
        return pltpu.make_async_remote_copy(
            src_ref=sums_in.at[r, pl.ds(0, size - 1)],
            dst_ref=sums_in.at[r, pl.ds(0, size - 1)],
            send_sem=sums_send.at[r],
            recv_sem=sums_recv.at[r],
            device_id=along(*rounds[r], 1),
            device_id_type=MESH,
        )

    def exchange_end(r):
        place, size = rounds[r]
        sums_in[r, here[place]] = sums_out[r]
        exchange_all(r).wait_recv()
        return sum((sums_in[r, k] for k in range(1, size)), sums_in[r, 0])

    def exchange_sent(r):
        exchange_all(r).wait_send()

    gather, spread = len(rounds), len(rounds) + 1

    def plane_copy(r, source, target, device):
        return pltpu.make_async_remote_copy(
            src_ref=source,
            dst_ref=target,
            send_sem=sums_send.at[r],
            recv_sem=sums_recv.at[r],
            device_id=device,
            device_id_type=MESH,
        )

    def plane_all(r, count):
        part = sums_in.at[r, pl.ds(0, count)]
        return plane_copy(r, part, part, along(2, zs, 1))

    def planes_gather(sums):
        sums_out[gather] = sums

        @pl.when(z != HUB)
        def _():
            to = sums_in.at[gather, z]
            plane_copy(gather, sums_out.at[gather], to, at(x, y, HUB, core)).start()

    def planes_spread():
        @pl.when(z == HUB)
        def _():
            plane_all(gather, zs - 1).wait_recv()
            sums_in[gather, HUB] = sums_out[gather]
            total = sum((sums_in[gather, k] for k in range(1, zs)), sums_in[gather, 0])
            sums_out[spread] = total
            sums_in[spread, 0] = total
            for d in range(1, zs):
                to = sums_in.at[spread, 0]
                plane_copy(spread, sums_out.at[spread], to, along(2, zs, d)).start()

    def planes_end():
        @pl.when(z != HUB)
        def _():
            plane_all(spread, 1).wait_recv()

        return sums_in[spread, 0]

    def planes_sent():
        @pl.when(z == HUB)
        def _():
            plane_all(spread, zs - 1).wait_send()

        @pl.when(z != HUB)
        def _():
            plane_all(gather, 1).wait_send()

    factor = (1.0 - DECAY_RATE) / B

    def gram_left(r):
        if r == 0:
            loads[2].wait()
        at_rows = pl.ds(r * COLS, COLS)
        gram = jnp.zeros((COLS, B), F32)
        for s in range(QUARTERS):
            gram += lax.dot_general(
                grads[s, at_rows, :], grads[s], (((1,), (1,)), ((), ())), preferred_element_type=F32
            )
        new_left[at_rows, :] = DECAY_RATE * new_left[at_rows, :] + factor * gram

    def gram_right(r):
        if r == 0:
            loads[3].wait()
        at_rows = pl.ds(r * COLS, COLS)
        turned = grads[r].T
        for s in range(QUARTERS):
            at_cols = pl.ds(s * COLS, COLS)
            gram = jnp.dot(turned, grads[s], preferred_element_type=F32)
            new_right[at_rows, at_cols] = DECAY_RATE * new_right[at_rows, at_cols] + factor * gram

    direction_sum = jnp.zeros((8, LANES), F32)
    for s in range(QUARTERS - 1):
        direction_sum = multiply_right(s, direction_sum)
        if s > 0:
            back_own(s)
    direction_sum = multiply_right(QUARTERS - 1, direction_sum)
    exchange_start(0, jnp.concatenate([grad_sum, direction_sum], axis=0))
    back_on(0)
    back_own(QUARTERS - 1)
    gram_left(0)
    gram_left(1)
    back_on(1)
    gram_left(2)
    gram_left(3)
    back_on(2)
    rights = [functools.partial(gram_right, k) for k in range(4)]
    steps = [
        rights[0:2],
        rights[2:4] + [functools.partial(finish, 0), functools.partial(back_on, 3)],
        [],
    ]
    for r in range(len(rounds)):
        totals = exchange_end(r)
        if r + 1 < len(rounds):
            exchange_start(r + 1, totals)
        for step in steps[r]:
            step()
    for r in range(len(rounds), len(steps)):
        for step in steps[r]:
            step()
    if zs > 1:
        planes_gather(totals)
    finish(1)
    if zs > 1:
        planes_spread()
    finish(2)
    if zs > 1:
        totals = planes_end()
    grad_total = jnp.sum(totals[0:8], keepdims=True)
    direction_total = jnp.sum(totals[8:16], keepdims=True)
    scale[...] = jnp.broadcast_to(jnp.sqrt(grad_total / (direction_total + EPSILON)), (8, LANES))
    finish(3)

    for s in range(QUARTERS):
        all_sent(*there, s)
        all_sent(*back, s)
    for r in range(len(rounds)):
        exchange_sent(r)
    if zs > 1:
        planes_sent()


def store(wide, scale, left, right, update, new_left, new_right, narrow, sem):
    copies = [
        pltpu.make_async_copy(left, new_left, sem.at[0]),
        pltpu.make_async_copy(right, new_right, sem.at[1]),
    ]
    for copy in copies:
        copy.start()
    rows = PIECE * SUBROWS
    for k in range(HELD):
        part = pl.ds(k * rows, rows)
        narrow[part, :] = (scale[0:1, :] * wide[part, :]).astype(BF16)
        copies.append(pltpu.make_async_copy(narrow.at[part], update.at[part], sem.at[2 + k]))
        copies[-1].start()
    for copy in copies:
        copy.wait()


def local(sizes, gradient, block_position, block_owner, left_stats, right_stats, left_root, right_root):
    xs, ys, zs, cores = sizes
    rounds = sum(size > 1 for size in sizes) + 1
    held_rows = HELD * PIECE * SUBROWS
    outside = pl.BlockSpec(memory_space=pltpu.HBM)
    inside = pl.BlockSpec(memory_space=pltpu.VMEM)

    def quarters(*lead):
        return [pltpu.VMEM((*lead, PIECE, COLS), BF16)] * QUARTERS

    dma = pltpu.SemaphoreType.DMA
    results = pl.pallas_call(
        functools.partial(kernel, sizes),
        out_shape=(
            pltpu.VMEM((held_rows, LANES), F32),
            pltpu.VMEM((8, LANES), F32),
            pltpu.VMEM((B, B), F32),
            pltpu.VMEM((B, B), F32),
        ),
        in_specs=[outside] * 8,
        out_specs=(inside,) * 4,
        scratch_shapes=[
            pltpu.SMEM(block_position.shape, jnp.int32),
            pltpu.SMEM(block_owner.shape, jnp.int32),
            pltpu.SMEM((RING**GROUP_BLOCKS * RING * WORDS,), jnp.int32),
            pltpu.VMEM((held_rows, LANES), BF16),
            pltpu.VMEM((QUARTERS, B, COLS), BF16),
            pltpu.VMEM((OWNED, PIECE, B), BF16),
            pltpu.VMEM((B, B), BF16),
            pltpu.VMEM((B, B), BF16),
            pltpu.VMEM((OWNED, PIECE, COLS), F32),
            quarters(HELD),
            quarters(2 * SLOTS),
            quarters(2 * SLOTS),
            quarters(OWNED),
            quarters(2 * SLOTS),
            quarters(2 * SLOTS),
            pltpu.VMEM((rounds, 16, LANES), F32),
            pltpu.VMEM((rounds, 4, 16, LANES), F32),
            dma((7 + HELD,)),
            dma((QUARTERS,)),
            dma((QUARTERS, 4)),
            dma((QUARTERS,)),
            dma((QUARTERS, 4)),
            dma((rounds,)),
            dma((rounds,)),
        ],
        compiler_params=pltpu.CompilerParams(
            collective_id=0, has_side_effects=True, vmem_limit_bytes=32 * 1024 * 1024
        ),
        name="shampoo",
    )(
        *(
            pltpu.with_memory_space_constraint(value, pltpu.HBM)
            for value in (
                block_position,
                block_owner,
                jnp.asarray(tables()),
                gradient.reshape(held_rows, LANES),
                left_stats[0],
                right_stats[0],
                left_root[0].reshape(OWNED, PIECE, B),
                right_root[0],
            )
        )
    )
    update, new_left, new_right = pl.pallas_call(
        store,
        out_shape=(
            jax.ShapeDtypeStruct((held_rows, LANES), BF16),
            jax.ShapeDtypeStruct((B, B), F32),
            jax.ShapeDtypeStruct((B, B), F32),
        ),
        in_specs=[inside] * 4,
        out_specs=(outside,) * 3,
        scratch_shapes=[pltpu.VMEM((held_rows, LANES), BF16), dma((2 + HELD,))],
        compiler_params=pltpu.CompilerParams(vmem_limit_bytes=4 * 1024 * 1024),
        name="store",
    )(*(pltpu.with_memory_space_constraint(value, pltpu.VMEM) for value in results))
    return (update.reshape(-1), new_left[None], new_right[None])


def solution(mesh):
    cores = 2
    sizes = (mesh.shape["mp"] // RING, RING, mesh.shape["dp"] // cores, cores)
    split = P(("dp", "mp"))
    slots = P(("dp", "mp"), None, None)
    return jax.shard_map(
        functools.partial(local, sizes),
        mesh=mesh,
        in_specs=(split, P(), P(), slots, slots, slots, slots),
        out_specs=(split, slots, slots),
        check_vma=False,
    )
```

```python
import functools
import itertools

import jax
import jax.numpy as jnp
import numpy as np
from jax import lax
from jax.experimental import pallas as pl
from jax.experimental.pallas import tpu as pltpu
from jax.sharding import PartitionSpec as P

DECAY_RATE = 0.95
EPSILON = 1e-06
MESH = pl.DeviceIdType.MESH

RING = 4
GROUP_BLOCKS = 3
B = 1024
PIECE = 128
HELD = 6
OWNED = B // PIECE
COLS = 256
QUARTERS = B // COLS
SLOTS = 6
EARLY = 3
EARLIER = B - COLS
WORDS = 8
LANES = 128
HUB = 1
SUBROWS = B // LANES
F32, BF16 = jnp.float32, jnp.bfloat16


def schedule(wanted):
    ways = (1, RING - 1)
    far = [i for i in range(RING) if wanted[i][(i + 2) % RING]]
    best = None
    for split in itertools.product(*[range(len(wanted[i][(i + 2) % RING]) + 1) for i in far]):
        plus = dict(zip(far, split))
        first = {}
        for i in range(RING):
            pieces = wanted[i][(i + 2) % RING]
            n = plus.get(i, 0)
            first[i, 0], first[i, 1] = pieces[:n], pieces[n:]
        if max(len(p) for p in first.values()) > EARLY:
            continue
        loads = [
            len(first[i, w]) + len(first[(i - way) % RING, w]) + len(wanted[i][(i + way) % RING])
            for i in range(RING)
            for w, way in enumerate(ways)
        ]
        key = (max(loads), sum(v * v for v in loads))
        if best is None or key < best[0]:
            best = (key, first)
    assert best is not None and best[0][0] <= SLOTS
    first = best[1]
    sent = {}
    for i in range(RING):
        for w, way in enumerate(ways):
            slots = [None] * SLOTS
            for k, piece in enumerate(first[i, w]):
                slots[k] = ("own", piece)
            for k, piece in enumerate(first[(i - way) % RING, w]):
                slots[EARLY + k] = ("pass", piece)
            free = [t for t in range(SLOTS) if slots[t] is None]
            for t, piece in zip(free, wanted[i][(i + way) % RING]):
                slots[t] = ("own", piece)
            sent[i, w] = slots
    return sent


def packed(codes):
    return sum(int(c) << (5 * k) for k, c in enumerate(codes))


def tables():
    out = np.zeros((RING**GROUP_BLOCKS, RING, WORDS), np.int32)
    for owners in itertools.permutations(range(RING), GROUP_BLOCKS):
        row = (owners[0] * RING + owners[1]) * RING + owners[2]
        there = [[[] for _ in range(RING)] for _ in range(RING)]
        back = [[[] for _ in range(RING)] for _ in range(RING)]
        for piece in range(RING * HELD):
            holder, owner = piece // HELD, owners[piece // OWNED]
            there[holder][owner].append(piece)
            back[owner][holder].append(piece)
        for wanted, size, word in ((there, HELD, 0), (back, OWNED, 4)):
            sent = schedule(wanted)
            for i in range(RING):
                for w in range(2):
                    codes = []
                    for entry in sent[i, w]:
                        if entry is None:
                            codes.append(0)
                        elif entry[0] == "own":
                            codes.append(entry[1] % size)
                        else:
                            codes.append(size)
                    out[row, i, word + w] = packed(codes)
                arrived = {}
                for w, way in enumerate((1, RING - 1)):
                    for t, entry in enumerate(sent[(i - way) % RING, w]):
                        if entry is not None:
                            arrived[entry[1]] = size + w * SLOTS + t
                if word == 0:
                    codes = [HELD + 2 * SLOTS] * OWNED
                    if i in owners:
                        first = owners.index(i) * OWNED
                        for q in range(OWNED):
                            piece = first + q
                            mine = piece // HELD == i
                            codes[q] = piece % HELD if mine else arrived[piece]
                    out[row, i, 2] = packed(codes[:6])
                    out[row, i, 3] = packed(codes[6:])
                else:
                    codes = []
                    for k in range(HELD):
                        piece = i * HELD + k
                        mine = owners[piece // OWNED] == i
                        codes.append(piece % OWNED if mine else arrived[piece])
                    out[row, i, 6] = packed(codes)
    return out.reshape(-1)


def code(word, k):
    return lax.bitwise_and(lax.shift_right_logical(word, jnp.int32(5 * k)), jnp.int32(31))


def kernel(
    sizes,
    position_in,
    owner_in,
    table_in,
    gradient,
    left_stats,
    right_stats,
    left_root,
    right_root,
    wide,
    scale,
    new_left,
    new_right,
    position,
    owner,
    table,
    flat,
    grads,
    left,
    right,
    half,
    begun,
    own,
    there_out,
    there_in,
    product,
    back_out,
    back_in,
    sums_out,
    sums_in,
    local_sem,
    there_send,
    there_recv,
    back_send,
    back_recv,
    sums_send,
    sums_recv,
):
    xs, ys, zs, cores = sizes
    dp, mp = lax.axis_index("dp"), lax.axis_index("mp")
    z, core = dp // cores, dp % cores
    x, y = mp // ys, mp % ys

    def at(x, y, z, core):
        return (z * cores + core, x * ys + y)

    neighbours = (at(x, (y + 1) % ys, z, core), at(x, (y + ys - 1) % ys, z, core))

    here = (x, y, z, core)
    rounds = [(place, size) for place, size in ((1, ys), (3, cores), (0, xs)) if size > 1]

    def along(place, size, distance):
        there = list(here)
        there[place] = (here[place] + distance) % size
        return at(*there)

    greeted = [along(place, size, d) for place, size in rounds for d in range(1, size)]

    rows = PIECE * SUBROWS
    parts = [pl.ds(k * rows, rows) for k in range(HELD)]
    loads = [
        pltpu.make_async_copy(source, target, local_sem.at[k])
        for k, (source, target) in enumerate(
            (
                (left_root, left),
                (right_root, right),
                (left_stats, new_left),
                (right_stats, new_right),
                (position_in, position),
                (owner_in, owner),
                (table_in, table),
                *((gradient.at[part], flat.at[part]) for part in parts),
            )
        )
    ]
    for k in (4, 5, 6, *range(7, 7 + HELD), 0, 1, 2, 3):
        loads[k].start()

    barrier = pltpu.get_barrier_semaphore()
    for device in greeted:
        pl.semaphore_signal(barrier, inc=1, device_id=device, device_id_type=MESH)
    planes = len(greeted)
    if zs > 1:
        planes += jnp.where(z == HUB, zs - 1, 1)

        @pl.when(z == HUB)
        def _():
            for d in range(1, zs):
                pl.semaphore_signal(barrier, inc=1, device_id=along(2, zs, d), device_id_type=MESH)

        @pl.when(z != HUB)
        def _():
            pl.semaphore_signal(
                barrier, inc=1, device_id=at(x, y, HUB, core), device_id_type=MESH
            )


    group = (dp * (xs * ys) + mp) // RING

    def find(b, found):
        place, device = position[b], owner[b]
        return tuple(
            jnp.where(place == GROUP_BLOCKS * group + k, device, f) for k, f in enumerate(found)
        )

    for k in (4, 5, 6):
        loads[k].wait()
    zero = jnp.int32(0)
    found = lax.fori_loop(0, position.shape[0], find, (zero,) * GROUP_BLOCKS)
    row = zero
    for f in found:
        row = row * RING + (f - RING * group)
    row = jnp.clip(row, 0, RING**GROUP_BLOCKS - 1)
    base = (row * RING + y) * WORDS
    words = [table[base + k] for k in range(7)]

    for k, part in enumerate(parts):
        loads[7 + k].wait()
        wide[part, :] = flat[part, :].astype(F32)

    def take(s):
        for k in range(HELD):
            for h in range(COLS // LANES):
                start = k * rows + s * (COLS // LANES) + h
                block = wide[pl.ds(start, PIECE, stride=SUBROWS), :]
                own[s][k, :, h * LANES : (h + 1) * LANES] = block.astype(BF16)

    def copy_of(out, into, send, recv, s, w, late):
        slots = pl.ds(w * SLOTS + late * EARLY, EARLY)
        return pltpu.make_async_remote_copy(
            src_ref=out[s].at[slots],
            dst_ref=into[s].at[slots],
            send_sem=send.at[s],
            recv_sem=recv.at[s, late],
            device_id=neighbours[w],
            device_id_type=MESH,
        )

    def both_came(out, into, send, recv, s, late):
        slots = pl.ds(0, 2 * EARLY)
        pltpu.make_async_remote_copy(
            src_ref=out[s].at[slots],
            dst_ref=into[s].at[slots],
            send_sem=send.at[s],
            recv_sem=recv.at[s, late],
            device_id=neighbours[0],
            device_id_type=MESH,
        ).wait_recv()

    def send_own(out, into, send, recv, source, pair, size, s):
        for w in range(2):
            for t in range(EARLY):
                out[s][w * SLOTS + t] = source[s][jnp.minimum(code(pair[w], t), size - 1)]
            copy_of(out, into, send, recv, s, w, 0).start()

    def send_on(out, into, send, recv, source, pair, size, s):
        both_came(out, into, send, recv, s, 0)
        for w in range(2):
            for t in range(EARLY, SLOTS):
                c = code(pair[w], t)
                passed = into[s][w * SLOTS + t - EARLY]
                mine = source[s][jnp.minimum(c, size - 1)]
                out[s][w * SLOTS + t] = jnp.where(c == size, passed, mine)
            copy_of(out, into, send, recv, s, w, 1).start()

    def arrive(out, into, send, recv, s):
        both_came(out, into, send, recv, s, 1)

    def all_sent(out, into, send, recv, s):
        pltpu.make_async_remote_copy(
            src_ref=out[s],
            dst_ref=into[s],
            send_sem=send.at[s],
            recv_sem=recv.at[s, 0],
            device_id=neighbours[0],
            device_id_type=MESH,
        ).wait_send()

    def pick(source, into, c, size, s):
        mine = source[s][jnp.minimum(c, size - 1)]
        came = into[s][jnp.clip(c - size, 0, 2 * SLOTS - 1)]
        return jnp.where(c < size, mine, came)

    there = (there_out, there_in, there_send, there_recv)
    back = (back_out, back_in, back_send, back_recv)

    def there_own(s):
        take(s)
        send_own(*there, own, words[0:2], HELD, s)

    def there_on(s):
        send_on(*there, own, words[0:2], HELD, s)

    def assemble(s):
        arrive(*there, s)
        for q in range(OWNED):
            c = code(words[2 + q // 6], q % 6)
            value = pick(own, there_in, c, HELD, s)
            value = jnp.where(c < HELD + 2 * SLOTS, value, jnp.zeros_like(value))
            grads[s, pl.ds(q * PIECE, PIECE), :] = value

    def multiply_left(s):
        if s == 0:
            loads[0].wait()

        def tile(r, carry):
            at_rows = pl.ds(pl.multiple_of(r * COLS, COLS), COLS)
            roots = left[pl.ds(r * 2, 2)].reshape(COLS, B)
            part = jnp.dot(roots, grads[s], preferred_element_type=F32)
            half[at_rows, s * COLS : (s + 1) * COLS] = part.astype(BF16)
            return carry

        lax.fori_loop(0, B // COLS, tile, 0)

    def begin_right():
        loads[1].wait()

        def tile(r, carry):
            at_rows = pl.ds(pl.multiple_of(r * COLS, COLS), COLS)
            part = jnp.dot(
                half[at_rows, :EARLIER], right[:EARLIER, :COLS], preferred_element_type=F32
            )
            begun[pl.ds(r * 2, 2)] = part.reshape(2, PIECE, COLS)
            return carry

        lax.fori_loop(0, B // COLS, tile, 0)

    def back_first():
        last = QUARTERS - 1
        for t in range(EARLY):
            places = [jnp.minimum(code(words[4 + w], t), OWNED - 1) for w in range(2)]
            roots = jnp.concatenate([left[q] for q in places], axis=0)
            start = jnp.concatenate([begun[q] for q in places], axis=0)
            part = jnp.dot(roots, grads[last], preferred_element_type=F32).astype(BF16)
            part = jnp.dot(part, right[EARLIER:, :COLS], preferred_element_type=F32)
            part = (start + part).astype(BF16)
            for w in range(2):
                slot = w * SLOTS + t
                back_out[0][slot] = part[w * PIECE : (w + 1) * PIECE]
                pltpu.make_async_remote_copy(
                    src_ref=back_out[0].at[slot],
                    dst_ref=back_in[0].at[slot],
                    send_sem=back_send.at[0],
                    recv_sem=back_recv.at[0, 0],
                    device_id=neighbours[w],
                    device_id_type=MESH,
                ).start()

    pl.semaphore_wait(barrier, planes)
    there_own(0)
    there_own(1)
    there_own(2)
    grad_sum = jnp.zeros((8, LANES), F32)
    for part in parts:
        squares = jnp.square(wide[part, :])
        grad_sum += jnp.sum(squares.reshape(rows // 8, 8, LANES), axis=0)
    there_on(0)
    there_own(3)
    there_on(1)
    assemble(0)
    multiply_left(0)
    there_on(2)
    assemble(1)
    multiply_left(1)
    there_on(3)
    assemble(2)
    multiply_left(2)
    begin_right()
    assemble(3)
    back_first()
    multiply_left(3)

    def multiply_right(s, total):
        def tile(r, total):
            at_rows = pl.ds(pl.multiple_of(r * COLS, COLS), COLS)
            at_cols = pl.ds(s * COLS, COLS)
            if s == 0:
                part = jnp.dot(
                    half[at_rows, EARLIER:], right[EARLIER:, at_cols], preferred_element_type=F32
                )
                part = (begun[pl.ds(r * 2, 2)].reshape(COLS, COLS) + part).astype(BF16)
            else:
                part = jnp.dot(
                    half[at_rows, :], right[:, at_cols], preferred_element_type=F32
                ).astype(BF16)
            product[s][pl.ds(r * 2, 2)] = part.reshape(2, PIECE, COLS)
            squares = jnp.square(part.astype(F32))
            squares = squares[:, :LANES] + squares[:, LANES:]
            return total + jnp.sum(squares.reshape(COLS // 8, 8, LANES), axis=0)

        return lax.fori_loop(0, B // COLS, tile, total, unroll=True)

    def back_own(s):
        send_own(*back, product, words[4:6], OWNED, s)

    def back_on(s):
        send_on(*back, product, words[4:6], OWNED, s)

    def finish(s):
        arrive(*back, s)
        for k in range(HELD):
            value = pick(product, back_in, code(words[6], k), OWNED, s).astype(F32)
            for h in range(COLS // LANES):
                start = k * rows + s * (COLS // LANES) + h
                wide[pl.ds(start, PIECE, stride=SUBROWS), :] = value[:, h * LANES : (h + 1) * LANES]

    def exchange(r, d):
        place, size = rounds[r]
        return pltpu.make_async_remote_copy(
            src_ref=sums_out.at[r],
            dst_ref=sums_in.at[r, here[place]],
            send_sem=sums_send.at[r],
            recv_sem=sums_recv.at[r],
            device_id=along(place, size, d),
            device_id_type=MESH,
        )

    def exchange_start(r, sums):
        place, size = rounds[r]
        sums_out[r] = sums
        for d in range(1, size):
            exchange(r, d).start()

    def exchange_all(r):
        size = rounds[r][1]
        return pltpu.make_async_remote_copy(
            src_ref=sums_in.at[r, pl.ds(0, size - 1)],
            dst_ref=sums_in.at[r, pl.ds(0, size - 1)],
            send_sem=sums_send.at[r],
            recv_sem=sums_recv.at[r],
            device_id=along(*rounds[r], 1),
            device_id_type=MESH,
        )

    def exchange_end(r):
        place, size = rounds[r]
        sums_in[r, here[place]] = sums_out[r]
        exchange_all(r).wait_recv()
        return sum((sums_in[r, k] for k in range(1, size)), sums_in[r, 0])

    def exchange_sent(r):
        exchange_all(r).wait_send()

    gather, spread = len(rounds), len(rounds) + 1

    def plane_copy(r, source, target, device):
        return pltpu.make_async_remote_copy(
            src_ref=source,
            dst_ref=target,
            send_sem=sums_send.at[r],
            recv_sem=sums_recv.at[r],
            device_id=device,
            device_id_type=MESH,
        )

    def plane_all(r, count):
        part = sums_in.at[r, pl.ds(0, count)]
        return plane_copy(r, part, part, along(2, zs, 1))

    def planes_gather(sums):
        sums_out[gather] = sums

        @pl.when(z != HUB)
        def _():
            to = sums_in.at[gather, z]
            plane_copy(gather, sums_out.at[gather], to, at(x, y, HUB, core)).start()

    def planes_spread():
        @pl.when(z == HUB)
        def _():
            plane_all(gather, zs - 1).wait_recv()
            sums_in[gather, HUB] = sums_out[gather]
            total = sum((sums_in[gather, k] for k in range(1, zs)), sums_in[gather, 0])
            sums_out[spread] = total
            sums_in[spread, 0] = total
            for d in range(1, zs):
                to = sums_in.at[spread, 0]
                plane_copy(spread, sums_out.at[spread], to, along(2, zs, d)).start()

    def planes_end():
        @pl.when(z != HUB)
        def _():
            plane_all(spread, 1).wait_recv()

        return sums_in[spread, 0]

    def planes_sent():
        @pl.when(z == HUB)
        def _():
            plane_all(spread, zs - 1).wait_send()

        @pl.when(z != HUB)
        def _():
            plane_all(gather, 1).wait_send()

    factor = (1.0 - DECAY_RATE) / B

    def gram_left(r):
        if r == 0:
            loads[2].wait()
        at_rows = pl.ds(r * COLS, COLS)
        gram = jnp.zeros((COLS, B), F32)
        for s in range(QUARTERS):
            gram += lax.dot_general(
                grads[s, at_rows, :], grads[s], (((1,), (1,)), ((), ())), preferred_element_type=F32
            )
        new_left[at_rows, :] = DECAY_RATE * new_left[at_rows, :] + factor * gram

    def gram_right(r):
        if r == 0:
            loads[3].wait()
        at_rows = pl.ds(r * COLS, COLS)
        turned = grads[r].T
        for s in range(QUARTERS):
            at_cols = pl.ds(s * COLS, COLS)
            gram = jnp.dot(turned, grads[s], preferred_element_type=F32)
            new_right[at_rows, at_cols] = DECAY_RATE * new_right[at_rows, at_cols] + factor * gram

    direction_sum = jnp.zeros((8, LANES), F32)
    for s in range(QUARTERS - 1):
        direction_sum = multiply_right(s, direction_sum)
        if s > 0:
            back_own(s)
    direction_sum = multiply_right(QUARTERS - 1, direction_sum)
    exchange_start(0, jnp.concatenate([grad_sum, direction_sum], axis=0))
    back_on(0)
    back_own(QUARTERS - 1)
    gram_left(0)
    gram_left(1)
    back_on(1)
    gram_left(2)
    gram_left(3)
    back_on(2)
    rights = [functools.partial(gram_right, k) for k in range(4)]
    steps = [
        rights[0:2],
        rights[2:4] + [functools.partial(finish, 0), functools.partial(back_on, 3)],
        [],
    ]
    for r in range(len(rounds)):
        totals = exchange_end(r)
        if r + 1 < len(rounds):
            exchange_start(r + 1, totals)
        for step in steps[r]:
            step()
    for r in range(len(rounds), len(steps)):
        for step in steps[r]:
            step()
    if zs > 1:
        planes_gather(totals)
    finish(1)
    if zs > 1:
        planes_spread()
    finish(2)
    if zs > 1:
        totals = planes_end()
    grad_total = jnp.sum(totals[0:8], keepdims=True)
    direction_total = jnp.sum(totals[8:16], keepdims=True)
    scale[...] = jnp.broadcast_to(jnp.sqrt(grad_total / (direction_total + EPSILON)), (8, LANES))
    finish(3)

    for s in range(QUARTERS):
        all_sent(*there, s)
        all_sent(*back, s)
    for r in range(len(rounds)):
        exchange_sent(r)
    if zs > 1:
        planes_sent()


def store(wide, scale, left, right, update, new_left, new_right, narrow, sem):
    copies = [
        pltpu.make_async_copy(left, new_left, sem.at[0]),
        pltpu.make_async_copy(right, new_right, sem.at[1]),
    ]
    for copy in copies:
        copy.start()
    rows = PIECE * SUBROWS
    for k in range(HELD):
        part = pl.ds(k * rows, rows)
        narrow[part, :] = (scale[0:1, :] * wide[part, :]).astype(BF16)
        copies.append(pltpu.make_async_copy(narrow.at[part], update.at[part], sem.at[2 + k]))
        copies[-1].start()
    for copy in copies:
        copy.wait()


def local(sizes, gradient, block_position, block_owner, left_stats, right_stats, left_root, right_root):
    xs, ys, zs, cores = sizes
    rounds = sum(size > 1 for size in sizes) + 1
    held_rows = HELD * PIECE * SUBROWS
    outside = pl.BlockSpec(memory_space=pltpu.HBM)
    inside = pl.BlockSpec(memory_space=pltpu.VMEM)

    def quarters(*lead):
        return [pltpu.VMEM((*lead, PIECE, COLS), BF16)] * QUARTERS

    dma = pltpu.SemaphoreType.DMA
    results = pl.pallas_call(
        functools.partial(kernel, sizes),
        out_shape=(
            pltpu.VMEM((held_rows, LANES), F32),
            pltpu.VMEM((8, LANES), F32),
            pltpu.VMEM((B, B), F32),
            pltpu.VMEM((B, B), F32),
        ),
        in_specs=[outside] * 8,
        out_specs=(inside,) * 4,
        scratch_shapes=[
            pltpu.SMEM(block_position.shape, jnp.int32),
            pltpu.SMEM(block_owner.shape, jnp.int32),
            pltpu.SMEM((RING**GROUP_BLOCKS * RING * WORDS,), jnp.int32),
            pltpu.VMEM((held_rows, LANES), BF16),
            pltpu.VMEM((QUARTERS, B, COLS), BF16),
            pltpu.VMEM((OWNED, PIECE, B), BF16),
            pltpu.VMEM((B, B), BF16),
            pltpu.VMEM((B, B), BF16),
            pltpu.VMEM((OWNED, PIECE, COLS), F32),
            quarters(HELD),
            quarters(2 * SLOTS),
            quarters(2 * SLOTS),
            quarters(OWNED),
            quarters(2 * SLOTS),
            quarters(2 * SLOTS),
            pltpu.VMEM((rounds, 16, LANES), F32),
            pltpu.VMEM((rounds, 4, 16, LANES), F32),
            dma((7 + HELD,)),
            dma((QUARTERS,)),
            dma((QUARTERS, 2)),
            dma((QUARTERS,)),
            dma((QUARTERS, 2)),
            dma((rounds,)),
            dma((rounds,)),
        ],
        compiler_params=pltpu.CompilerParams(
            collective_id=0, has_side_effects=True, vmem_limit_bytes=32 * 1024 * 1024
        ),
        name="shampoo",
    )(
        *(
            pltpu.with_memory_space_constraint(value, pltpu.HBM)
            for value in (
                block_position,
                block_owner,
                jnp.asarray(tables()),
                gradient.reshape(held_rows, LANES),
                left_stats[0],
                right_stats[0],
                left_root[0].reshape(OWNED, PIECE, B),
                right_root[0],
            )
        )
    )
    update, new_left, new_right = pl.pallas_call(
        store,
        out_shape=(
            jax.ShapeDtypeStruct((held_rows, LANES), BF16),
            jax.ShapeDtypeStruct((B, B), F32),
            jax.ShapeDtypeStruct((B, B), F32),
        ),
        in_specs=[inside] * 4,
        out_specs=(outside,) * 3,
        scratch_shapes=[pltpu.VMEM((held_rows, LANES), BF16), dma((2 + HELD,))],
        compiler_params=pltpu.CompilerParams(vmem_limit_bytes=4 * 1024 * 1024),
        name="store",
    )(*(pltpu.with_memory_space_constraint(value, pltpu.VMEM) for value in results))
    return (update.reshape(-1), new_left[None], new_right[None])


def solution(mesh):
    cores = 2
    sizes = (mesh.shape["mp"] // RING, RING, mesh.shape["dp"] // cores, cores)
    split = P(("dp", "mp"))
    slots = P(("dp", "mp"), None, None)
    return jax.shard_map(
        functools.partial(local, sizes),
        mesh=mesh,
        in_specs=(split, P(), P(), slots, slots, slots, slots),
        out_specs=(split, slots, slots),
        check_vma=False,
    )
```

```python
import functools
import itertools

import jax
import jax.numpy as jnp
import numpy as np
from jax import lax
from jax.experimental import pallas as pl
from jax.experimental.pallas import tpu as pltpu
from jax.sharding import PartitionSpec as P

DECAY_RATE = 0.95
EPSILON = 1e-06
MESH = pl.DeviceIdType.MESH

RING = 4
GROUP_BLOCKS = 3
B = 1024
PIECE = 128
HELD = 6
OWNED = B // PIECE
COLS = 256
QUARTERS = B // COLS
SLOTS = 6
EARLY = 3
EARLIER = B - COLS
WORDS = 8
LANES = 128
HUB = 1
SUBROWS = B // LANES
F32, BF16 = jnp.float32, jnp.bfloat16


def schedule(wanted):
    ways = (1, RING - 1)
    far = [i for i in range(RING) if wanted[i][(i + 2) % RING]]
    best = None
    for split in itertools.product(*[range(len(wanted[i][(i + 2) % RING]) + 1) for i in far]):
        plus = dict(zip(far, split))
        first = {}
        for i in range(RING):
            pieces = wanted[i][(i + 2) % RING]
            n = plus.get(i, 0)
            first[i, 0], first[i, 1] = pieces[:n], pieces[n:]
        if max(len(p) for p in first.values()) > EARLY:
            continue
        loads = [
            len(first[i, w]) + len(first[(i - way) % RING, w]) + len(wanted[i][(i + way) % RING])
            for i in range(RING)
            for w, way in enumerate(ways)
        ]
        key = (max(loads), sum(v * v for v in loads))
        if best is None or key < best[0]:
            best = (key, first)
    assert best is not None and best[0][0] <= SLOTS
    first = best[1]
    sent = {}
    for i in range(RING):
        for w, way in enumerate(ways):
            slots = [None] * SLOTS
            for k, piece in enumerate(first[i, w]):
                slots[k] = ("own", piece)
            for k, piece in enumerate(first[(i - way) % RING, w]):
                slots[EARLY + k] = ("pass", piece)
            free = [t for t in range(SLOTS) if slots[t] is None]
            for t, piece in zip(free, wanted[i][(i + way) % RING]):
                slots[t] = ("own", piece)
            sent[i, w] = slots
    return sent


def packed(codes):
    return sum(int(c) << (5 * k) for k, c in enumerate(codes))


def tables():
    out = np.zeros((RING**GROUP_BLOCKS, RING, WORDS), np.int32)
    for owners in itertools.permutations(range(RING), GROUP_BLOCKS):
        row = (owners[0] * RING + owners[1]) * RING + owners[2]
        there = [[[] for _ in range(RING)] for _ in range(RING)]
        back = [[[] for _ in range(RING)] for _ in range(RING)]
        for piece in range(RING * HELD):
            holder, owner = piece // HELD, owners[piece // OWNED]
            there[holder][owner].append(piece)
            back[owner][holder].append(piece)
        for wanted, size, word in ((there, HELD, 0), (back, OWNED, 4)):
            sent = schedule(wanted)
            for i in range(RING):
                for w in range(2):
                    codes = []
                    for entry in sent[i, w]:
                        if entry is None:
                            codes.append(0)
                        elif entry[0] == "own":
                            codes.append(entry[1] % size)
                        else:
                            codes.append(size)
                    out[row, i, word + w] = packed(codes)
                arrived = {}
                for w, way in enumerate((1, RING - 1)):
                    for t, entry in enumerate(sent[(i - way) % RING, w]):
                        if entry is not None:
                            arrived[entry[1]] = size + w * SLOTS + t
                if word == 0:
                    codes = [HELD + 2 * SLOTS] * OWNED
                    if i in owners:
                        first = owners.index(i) * OWNED
                        for q in range(OWNED):
                            piece = first + q
                            mine = piece // HELD == i
                            codes[q] = piece % HELD if mine else arrived[piece]
                    out[row, i, 2] = packed(codes[:6])
                    out[row, i, 3] = packed(codes[6:])
                else:
                    codes = []
                    for k in range(HELD):
                        piece = i * HELD + k
                        mine = owners[piece // OWNED] == i
                        codes.append(piece % OWNED if mine else arrived[piece])
                    out[row, i, 6] = packed(codes)
    return out.reshape(-1)


def code(word, k):
    return lax.bitwise_and(lax.shift_right_logical(word, jnp.int32(5 * k)), jnp.int32(31))


def kernel(
    sizes,
    position_in,
    owner_in,
    table_in,
    gradient,
    left_stats,
    right_stats,
    left_root,
    right_root,
    wide,
    scale,
    new_left,
    new_right,
    position,
    owner,
    table,
    flat,
    grads,
    left,
    right,
    half,
    begun,
    own,
    there_out,
    there_in,
    product,
    back_out,
    back_in,
    sums_out,
    sums_in,
    local_sem,
    there_send,
    there_recv,
    back_send,
    back_recv,
    sums_send,
    sums_recv,
):
    xs, ys, zs, cores = sizes
    dp, mp = lax.axis_index("dp"), lax.axis_index("mp")
    z, core = dp // cores, dp % cores
    x, y = mp // ys, mp % ys

    def at(x, y, z, core):
        return (z * cores + core, x * ys + y)

    neighbours = (at(x, (y + 1) % ys, z, core), at(x, (y + ys - 1) % ys, z, core))

    here = (x, y, z, core)
    rounds = [(place, size) for place, size in ((1, ys), (3, cores), (0, xs)) if size > 1]

    def along(place, size, distance):
        there = list(here)
        there[place] = (here[place] + distance) % size
        return at(*there)

    greeted = [along(place, size, d) for place, size in rounds for d in range(1, size)]

    rows = PIECE * SUBROWS
    parts = [pl.ds(k * rows, rows) for k in range(HELD)]
    loads = [
        pltpu.make_async_copy(source, target, local_sem.at[k])
        for k, (source, target) in enumerate(
            (
                (left_root, left),
                (right_root, right),
                (left_stats, new_left),
                (right_stats, new_right),
                (position_in, position),
                (owner_in, owner),
                (table_in, table),
                *((gradient.at[part], flat.at[part]) for part in parts),
            )
        )
    ]
    for k in (4, 5, 6, *range(7, 7 + HELD), 0, 1, 2, 3):
        loads[k].start()

    barrier = pltpu.get_barrier_semaphore()
    for device in greeted:
        pl.semaphore_signal(barrier, inc=1, device_id=device, device_id_type=MESH)
    planes = len(greeted)
    if zs > 1:
        planes += jnp.where(z == HUB, zs - 1, 1)

        @pl.when(z == HUB)
        def _():
            for d in range(1, zs):
                pl.semaphore_signal(barrier, inc=1, device_id=along(2, zs, d), device_id_type=MESH)

        @pl.when(z != HUB)
        def _():
            pl.semaphore_signal(
                barrier, inc=1, device_id=at(x, y, HUB, core), device_id_type=MESH
            )


    group = (dp * (xs * ys) + mp) // RING

    def find(b, found):
        place, device = position[b], owner[b]
        return tuple(
            jnp.where(place == GROUP_BLOCKS * group + k, device, f) for k, f in enumerate(found)
        )

    for k in (4, 5, 6):
        loads[k].wait()
    zero = jnp.int32(0)
    found = lax.fori_loop(0, position.shape[0], find, (zero,) * GROUP_BLOCKS)
    row = zero
    for f in found:
        row = row * RING + (f - RING * group)
    row = jnp.clip(row, 0, RING**GROUP_BLOCKS - 1)
    base = (row * RING + y) * WORDS
    words = [table[base + k] for k in range(7)]

    for k, part in enumerate(parts):
        loads[7 + k].wait()
        wide[part, :] = flat[part, :].astype(F32)

    def take(s):
        for k in range(HELD):
            for h in range(COLS // LANES):
                start = k * rows + s * (COLS // LANES) + h
                block = wide[pl.ds(start, PIECE, stride=SUBROWS), :]
                own[s][k, :, h * LANES : (h + 1) * LANES] = block.astype(BF16)

    def copy_of(out, into, send, recv, s, w, late):
        slots = pl.ds(w * SLOTS + late * EARLY, EARLY)
        return pltpu.make_async_remote_copy(
            src_ref=out[s].at[slots],
            dst_ref=into[s].at[slots],
            send_sem=send.at[s],
            recv_sem=recv.at[s, late],
            device_id=neighbours[w],
            device_id_type=MESH,
        )

    def both_came(out, into, send, recv, s, late):
        slots = pl.ds(0, 2 * EARLY)
        pltpu.make_async_remote_copy(
            src_ref=out[s].at[slots],
            dst_ref=into[s].at[slots],
            send_sem=send.at[s],
            recv_sem=recv.at[s, late],
            device_id=neighbours[0],
            device_id_type=MESH,
        ).wait_recv()

    def fill_own(out, source, pair, size, s, w):
        for t in range(EARLY):
            out[s][w * SLOTS + t] = source[s][jnp.minimum(code(pair[w], t), size - 1)]

    def send_own(out, into, send, recv, source, pair, size, s):
        for w in range(2):
            fill_own(out, source, pair, size, s, w)
            copy_of(out, into, send, recv, s, w, 0).start()

    def send_on(out, into, send, recv, source, pair, size, s):
        both_came(out, into, send, recv, s, 0)
        for w in range(2):
            for t in range(EARLY, SLOTS):
                c = code(pair[w], t)
                passed = into[s][w * SLOTS + t - EARLY]
                mine = source[s][jnp.minimum(c, size - 1)]
                out[s][w * SLOTS + t] = jnp.where(c == size, passed, mine)
            copy_of(out, into, send, recv, s, w, 1).start()

    def arrive(out, into, send, recv, s):
        both_came(out, into, send, recv, s, 1)

    def all_sent(out, into, send, recv, s):
        pltpu.make_async_remote_copy(
            src_ref=out[s],
            dst_ref=into[s],
            send_sem=send.at[s],
            recv_sem=recv.at[s, 0],
            device_id=neighbours[0],
            device_id_type=MESH,
        ).wait_send()

    def pick(source, into, c, size, s):
        mine = source[s][jnp.minimum(c, size - 1)]
        came = into[s][jnp.clip(c - size, 0, 2 * SLOTS - 1)]
        return jnp.where(c < size, mine, came)

    there = (there_out, there_in, there_send, there_recv)
    back = (back_out, back_in, back_send, back_recv)

    def there_own(s):
        take(s)
        send_own(*there, own, words[0:2], HELD, s)

    def there_on(s):
        send_on(*there, own, words[0:2], HELD, s)

    def assemble(s):
        arrive(*there, s)
        for q in range(OWNED):
            c = code(words[2 + q // 6], q % 6)
            value = pick(own, there_in, c, HELD, s)
            value = jnp.where(c < HELD + 2 * SLOTS, value, jnp.zeros_like(value))
            grads[s, pl.ds(q * PIECE, PIECE), :] = value

    def multiply_left(s):
        if s == 0:
            loads[0].wait()

        def tile(r, carry):
            at_rows = pl.ds(pl.multiple_of(r * COLS, COLS), COLS)
            roots = left[pl.ds(r * 2, 2)].reshape(COLS, B)
            part = jnp.dot(roots, grads[s], preferred_element_type=F32)
            half[at_rows, s * COLS : (s + 1) * COLS] = part.astype(BF16)
            return carry

        lax.fori_loop(0, B // COLS, tile, 0)

    def begin_right():
        loads[1].wait()

        def tile(r, carry):
            at_rows = pl.ds(pl.multiple_of(r * COLS, COLS), COLS)
            part = jnp.dot(
                half[at_rows, :EARLIER], right[:EARLIER, :COLS], preferred_element_type=F32
            )
            begun[pl.ds(r * 2, 2)] = part.reshape(2, PIECE, COLS)
            return carry

        lax.fori_loop(0, B // COLS, tile, 0)

    def back_first():
        last = QUARTERS - 1
        for t in range(EARLY):
            places = [jnp.minimum(code(words[4 + w], t), OWNED - 1) for w in range(2)]
            roots = jnp.concatenate([left[q] for q in places], axis=0)
            start = jnp.concatenate([begun[q] for q in places], axis=0)
            part = jnp.dot(roots, grads[last], preferred_element_type=F32).astype(BF16)
            part = jnp.dot(part, right[EARLIER:, :COLS], preferred_element_type=F32)
            part = (start + part).astype(BF16)
            for w in range(2):
                slot = w * SLOTS + t
                back_out[0][slot] = part[w * PIECE : (w + 1) * PIECE]
                pltpu.make_async_remote_copy(
                    src_ref=back_out[0].at[slot],
                    dst_ref=back_in[0].at[slot],
                    send_sem=back_send.at[0],
                    recv_sem=back_recv.at[0, 0],
                    device_id=neighbours[w],
                    device_id_type=MESH,
                ).start()

    take(0)
    for w in range(2):
        fill_own(there_out, own, words[0:2], HELD, 0, w)
    pl.semaphore_wait(barrier, planes)
    for w in range(2):
        copy_of(*there, 0, w, 0).start()
    there_own(1)
    there_own(2)
    grad_sum = jnp.zeros((8, LANES), F32)
    for part in parts:
        squares = jnp.square(wide[part, :])
        grad_sum += jnp.sum(squares.reshape(rows // 8, 8, LANES), axis=0)
    there_on(0)
    there_own(3)
    there_on(1)
    assemble(0)
    multiply_left(0)
    there_on(2)
    assemble(1)
    multiply_left(1)
    there_on(3)
    assemble(2)
    multiply_left(2)
    begin_right()
    assemble(3)
    back_first()
    multiply_left(3)

    def multiply_right(s, total):
        def tile(r, total):
            at_rows = pl.ds(pl.multiple_of(r * COLS, COLS), COLS)
            at_cols = pl.ds(s * COLS, COLS)
            if s == 0:
                part = jnp.dot(
                    half[at_rows, EARLIER:], right[EARLIER:, at_cols], preferred_element_type=F32
                )
                part = (begun[pl.ds(r * 2, 2)].reshape(COLS, COLS) + part).astype(BF16)
            else:
                part = jnp.dot(
                    half[at_rows, :], right[:, at_cols], preferred_element_type=F32
                ).astype(BF16)
            product[s][pl.ds(r * 2, 2)] = part.reshape(2, PIECE, COLS)
            squares = jnp.square(part.astype(F32))
            squares = squares[:, :LANES] + squares[:, LANES:]
            return total + jnp.sum(squares.reshape(COLS // 8, 8, LANES), axis=0)

        return lax.fori_loop(0, B // COLS, tile, total, unroll=True)

    def back_own(s):
        send_own(*back, product, words[4:6], OWNED, s)

    def back_on(s):
        send_on(*back, product, words[4:6], OWNED, s)

    def finish(s):
        arrive(*back, s)
        for k in range(HELD):
            value = pick(product, back_in, code(words[6], k), OWNED, s).astype(F32)
            for h in range(COLS // LANES):
                start = k * rows + s * (COLS // LANES) + h
                wide[pl.ds(start, PIECE, stride=SUBROWS), :] = value[:, h * LANES : (h + 1) * LANES]

    def exchange(r, d):
        place, size = rounds[r]
        return pltpu.make_async_remote_copy(
            src_ref=sums_out.at[r],
            dst_ref=sums_in.at[r, here[place]],
            send_sem=sums_send.at[r],
            recv_sem=sums_recv.at[r],
            device_id=along(place, size, d),
            device_id_type=MESH,
        )

    def exchange_start(r, sums):
        place, size = rounds[r]
        sums_out[r] = sums
        for d in range(1, size):
            exchange(r, d).start()

    def exchange_all(r):
        size = rounds[r][1]
        return pltpu.make_async_remote_copy(
            src_ref=sums_in.at[r, pl.ds(0, size - 1)],
            dst_ref=sums_in.at[r, pl.ds(0, size - 1)],
            send_sem=sums_send.at[r],
            recv_sem=sums_recv.at[r],
            device_id=along(*rounds[r], 1),
            device_id_type=MESH,
        )

    def exchange_end(r):
        place, size = rounds[r]
        sums_in[r, here[place]] = sums_out[r]
        exchange_all(r).wait_recv()
        return sum((sums_in[r, k] for k in range(1, size)), sums_in[r, 0])

    def exchange_sent(r):
        exchange_all(r).wait_send()

    gather, spread = len(rounds), len(rounds) + 1

    def plane_copy(r, source, target, device):
        return pltpu.make_async_remote_copy(
            src_ref=source,
            dst_ref=target,
            send_sem=sums_send.at[r],
            recv_sem=sums_recv.at[r],
            device_id=device,
            device_id_type=MESH,
        )

    def plane_all(r, count):
        part = sums_in.at[r, pl.ds(0, count)]
        return plane_copy(r, part, part, along(2, zs, 1))

    def planes_gather(sums):
        sums_out[gather] = sums

        @pl.when(z != HUB)
        def _():
            to = sums_in.at[gather, z]
            plane_copy(gather, sums_out.at[gather], to, at(x, y, HUB, core)).start()

    def planes_spread():
        @pl.when(z == HUB)
        def _():
            plane_all(gather, zs - 1).wait_recv()
            sums_in[gather, HUB] = sums_out[gather]
            total = sum((sums_in[gather, k] for k in range(1, zs)), sums_in[gather, 0])
            sums_out[spread] = total
            sums_in[spread, 0] = total
            for d in range(1, zs):
                to = sums_in.at[spread, 0]
                plane_copy(spread, sums_out.at[spread], to, along(2, zs, d)).start()

    def planes_end():
        @pl.when(z != HUB)
        def _():
            plane_all(spread, 1).wait_recv()

        return sums_in[spread, 0]

    def planes_sent():
        @pl.when(z == HUB)
        def _():
            plane_all(spread, zs - 1).wait_send()

        @pl.when(z != HUB)
        def _():
            plane_all(gather, 1).wait_send()

    factor = (1.0 - DECAY_RATE) / B

    def gram_left(r):
        if r == 0:
            loads[2].wait()
        at_rows = pl.ds(r * COLS, COLS)
        gram = jnp.zeros((COLS, B), F32)
        for s in range(QUARTERS):
            gram += lax.dot_general(
                grads[s, at_rows, :], grads[s], (((1,), (1,)), ((), ())), preferred_element_type=F32
            )
        new_left[at_rows, :] = DECAY_RATE * new_left[at_rows, :] + factor * gram

    def gram_right(r):
        if r == 0:
            loads[3].wait()
        at_rows = pl.ds(r * COLS, COLS)
        turned = grads[r].T
        for s in range(QUARTERS):
            at_cols = pl.ds(s * COLS, COLS)
            gram = jnp.dot(turned, grads[s], preferred_element_type=F32)
            new_right[at_rows, at_cols] = DECAY_RATE * new_right[at_rows, at_cols] + factor * gram

    direction_sum = jnp.zeros((8, LANES), F32)
    for s in range(QUARTERS - 1):
        direction_sum = multiply_right(s, direction_sum)
        if s > 0:
            back_own(s)
    direction_sum = multiply_right(QUARTERS - 1, direction_sum)
    exchange_start(0, jnp.concatenate([grad_sum, direction_sum], axis=0))
    back_on(0)
    back_own(QUARTERS - 1)
    gram_left(0)
    gram_left(1)
    back_on(1)
    gram_left(2)
    gram_left(3)
    back_on(2)
    rights = [functools.partial(gram_right, k) for k in range(4)]
    steps = [
        rights[0:2],
        rights[2:4] + [functools.partial(finish, 0), functools.partial(back_on, 3)],
        [],
    ]
    for r in range(len(rounds)):
        totals = exchange_end(r)
        if r + 1 < len(rounds):
            exchange_start(r + 1, totals)
        for step in steps[r]:
            step()
    for r in range(len(rounds), len(steps)):
        for step in steps[r]:
            step()
    if zs > 1:
        planes_gather(totals)
    finish(1)
    if zs > 1:
        planes_spread()
    for s in range(QUARTERS):
        all_sent(*there, s)
    for r in range(len(rounds)):
        exchange_sent(r)
    finish(2)
    if zs > 1:
        totals = planes_end()
        planes_sent()
    grad_total = jnp.sum(totals[0:8], keepdims=True)
    direction_total = jnp.sum(totals[8:16], keepdims=True)
    scale[...] = jnp.broadcast_to(jnp.sqrt(grad_total / (direction_total + EPSILON)), (8, LANES))
    finish(3)

    for s in range(QUARTERS):
        all_sent(*back, s)


def store(wide, scale, left, right, update, new_left, new_right, narrow, sem):
    copies = [
        pltpu.make_async_copy(left, new_left, sem.at[0]),
        pltpu.make_async_copy(right, new_right, sem.at[1]),
    ]
    for copy in copies:
        copy.start()
    rows = PIECE * SUBROWS
    for k in range(HELD):
        part = pl.ds(k * rows, rows)
        narrow[part, :] = (scale[0:1, :] * wide[part, :]).astype(BF16)
        copies.append(pltpu.make_async_copy(narrow.at[part], update.at[part], sem.at[2 + k]))
        copies[-1].start()
    for copy in copies:
        copy.wait()


def local(sizes, gradient, block_position, block_owner, left_stats, right_stats, left_root, right_root):
    xs, ys, zs, cores = sizes
    rounds = sum(size > 1 for size in sizes) + 1
    held_rows = HELD * PIECE * SUBROWS
    outside = pl.BlockSpec(memory_space=pltpu.HBM)
    inside = pl.BlockSpec(memory_space=pltpu.VMEM)

    def quarters(*lead):
        return [pltpu.VMEM((*lead, PIECE, COLS), BF16)] * QUARTERS

    dma = pltpu.SemaphoreType.DMA
    results = pl.pallas_call(
        functools.partial(kernel, sizes),
        out_shape=(
            pltpu.VMEM((held_rows, LANES), F32),
            pltpu.VMEM((8, LANES), F32),
            pltpu.VMEM((B, B), F32),
            pltpu.VMEM((B, B), F32),
        ),
        in_specs=[outside] * 8,
        out_specs=(inside,) * 4,
        scratch_shapes=[
            pltpu.SMEM(block_position.shape, jnp.int32),
            pltpu.SMEM(block_owner.shape, jnp.int32),
            pltpu.SMEM((RING**GROUP_BLOCKS * RING * WORDS,), jnp.int32),
            pltpu.VMEM((held_rows, LANES), BF16),
            pltpu.VMEM((QUARTERS, B, COLS), BF16),
            pltpu.VMEM((OWNED, PIECE, B), BF16),
            pltpu.VMEM((B, B), BF16),
            pltpu.VMEM((B, B), BF16),
            pltpu.VMEM((OWNED, PIECE, COLS), F32),
            quarters(HELD),
            quarters(2 * SLOTS),
            quarters(2 * SLOTS),
            quarters(OWNED),
            quarters(2 * SLOTS),
            quarters(2 * SLOTS),
            pltpu.VMEM((rounds, 16, LANES), F32),
            pltpu.VMEM((rounds, 4, 16, LANES), F32),
            dma((7 + HELD,)),
            dma((QUARTERS,)),
            dma((QUARTERS, 2)),
            dma((QUARTERS,)),
            dma((QUARTERS, 2)),
            dma((rounds,)),
            dma((rounds,)),
        ],
        compiler_params=pltpu.CompilerParams(
            collective_id=0, has_side_effects=True, vmem_limit_bytes=32 * 1024 * 1024
        ),
        name="shampoo",
    )(
        *(
            pltpu.with_memory_space_constraint(value, pltpu.HBM)
            for value in (
                block_position,
                block_owner,
                jnp.asarray(tables()),
                gradient.reshape(held_rows, LANES),
                left_stats[0],
                right_stats[0],
                left_root[0].reshape(OWNED, PIECE, B),
                right_root[0],
            )
        )
    )
    update, new_left, new_right = pl.pallas_call(
        store,
        out_shape=(
            jax.ShapeDtypeStruct((held_rows, LANES), BF16),
            jax.ShapeDtypeStruct((B, B), F32),
            jax.ShapeDtypeStruct((B, B), F32),
        ),
        in_specs=[inside] * 4,
        out_specs=(outside,) * 3,
        scratch_shapes=[pltpu.VMEM((held_rows, LANES), BF16), dma((2 + HELD,))],
        compiler_params=pltpu.CompilerParams(vmem_limit_bytes=4 * 1024 * 1024),
        name="store",
    )(*(pltpu.with_memory_space_constraint(value, pltpu.VMEM) for value in results))
    return (update.reshape(-1), new_left[None], new_right[None])


def solution(mesh):
    cores = 2
    sizes = (mesh.shape["mp"] // RING, RING, mesh.shape["dp"] // cores, cores)
    split = P(("dp", "mp"))
    slots = P(("dp", "mp"), None, None)
    return jax.shard_map(
        functools.partial(local, sizes),
        mesh=mesh,
        in_specs=(split, P(), P(), slots, slots, slots, slots),
        out_specs=(split, slots, slots),
        check_vma=False,
    )
```

```python
import functools
import itertools

import jax
import jax.numpy as jnp
import numpy as np
from jax import lax
from jax.experimental import pallas as pl
from jax.experimental.pallas import tpu as pltpu
from jax.sharding import PartitionSpec as P

DECAY_RATE = 0.95
EPSILON = 1e-06
MESH = pl.DeviceIdType.MESH

RING = 4
GROUP_BLOCKS = 3
B = 1024
PIECE = 128
HELD = 6
OWNED = B // PIECE
COLS = 256
QUARTERS = B // COLS
SLOTS = 6
EARLY = 3
EARLIER = B - COLS
WORDS = 8
LANES = 128
STORES = 2
HUB = 1
SUBROWS = B // LANES
F32, BF16 = jnp.float32, jnp.bfloat16


def schedule(wanted):
    ways = (1, RING - 1)
    far = [i for i in range(RING) if wanted[i][(i + 2) % RING]]
    best = None
    for split in itertools.product(*[range(len(wanted[i][(i + 2) % RING]) + 1) for i in far]):
        plus = dict(zip(far, split))
        first = {}
        for i in range(RING):
            pieces = wanted[i][(i + 2) % RING]
            n = plus.get(i, 0)
            first[i, 0], first[i, 1] = pieces[:n], pieces[n:]
        if max(len(p) for p in first.values()) > EARLY:
            continue
        loads = [
            len(first[i, w]) + len(first[(i - way) % RING, w]) + len(wanted[i][(i + way) % RING])
            for i in range(RING)
            for w, way in enumerate(ways)
        ]
        key = (max(loads), sum(v * v for v in loads))
        if best is None or key < best[0]:
            best = (key, first)
    assert best is not None and best[0][0] <= SLOTS
    first = best[1]
    sent = {}
    for i in range(RING):
        for w, way in enumerate(ways):
            slots = [None] * SLOTS
            for k, piece in enumerate(first[i, w]):
                slots[k] = ("own", piece)
            for k, piece in enumerate(first[(i - way) % RING, w]):
                slots[EARLY + k] = ("pass", piece)
            free = [t for t in range(SLOTS) if slots[t] is None]
            for t, piece in zip(free, wanted[i][(i + way) % RING]):
                slots[t] = ("own", piece)
            sent[i, w] = slots
    return sent


def packed(codes):
    return sum(int(c) << (5 * k) for k, c in enumerate(codes))


def tables():
    out = np.zeros((RING**GROUP_BLOCKS, RING, WORDS), np.int32)
    for owners in itertools.permutations(range(RING), GROUP_BLOCKS):
        row = (owners[0] * RING + owners[1]) * RING + owners[2]
        there = [[[] for _ in range(RING)] for _ in range(RING)]
        back = [[[] for _ in range(RING)] for _ in range(RING)]
        for piece in range(RING * HELD):
            holder, owner = piece // HELD, owners[piece // OWNED]
            there[holder][owner].append(piece)
            back[owner][holder].append(piece)
        for wanted, size, word in ((there, HELD, 0), (back, OWNED, 4)):
            sent = schedule(wanted)
            for i in range(RING):
                for w in range(2):
                    codes = []
                    for entry in sent[i, w]:
                        if entry is None:
                            codes.append(0)
                        elif entry[0] == "own":
                            codes.append(entry[1] % size)
                        else:
                            codes.append(size)
                    out[row, i, word + w] = packed(codes)
                arrived = {}
                for w, way in enumerate((1, RING - 1)):
                    for t, entry in enumerate(sent[(i - way) % RING, w]):
                        if entry is not None:
                            arrived[entry[1]] = size + w * SLOTS + t
                if word == 0:
                    codes = [HELD + 2 * SLOTS] * OWNED
                    if i in owners:
                        first = owners.index(i) * OWNED
                        for q in range(OWNED):
                            piece = first + q
                            mine = piece // HELD == i
                            codes[q] = piece % HELD if mine else arrived[piece]
                    out[row, i, 2] = packed(codes[:6])
                    out[row, i, 3] = packed(codes[6:])
                else:
                    codes = []
                    for k in range(HELD):
                        piece = i * HELD + k
                        mine = owners[piece // OWNED] == i
                        codes.append(piece % OWNED if mine else arrived[piece])
                    out[row, i, 6] = packed(codes)
    return out.reshape(-1)


def code(word, k):
    return lax.bitwise_and(lax.shift_right_logical(word, jnp.int32(5 * k)), jnp.int32(31))


def kernel(
    sizes,
    position_in,
    owner_in,
    table_in,
    gradient,
    left_stats,
    right_stats,
    left_root,
    right_root,
    wide,
    scale,
    new_left,
    new_right,
    position,
    owner,
    table,
    flat,
    grads,
    left,
    right,
    half,
    begun,
    own,
    there_out,
    there_in,
    product,
    back_out,
    back_in,
    sums_out,
    sums_in,
    local_sem,
    there_send,
    there_recv,
    back_send,
    back_recv,
    sums_send,
    sums_recv,
):
    xs, ys, zs, cores = sizes
    dp, mp = lax.axis_index("dp"), lax.axis_index("mp")
    z, core = dp // cores, dp % cores
    x, y = mp // ys, mp % ys

    def at(x, y, z, core):
        return (z * cores + core, x * ys + y)

    neighbours = (at(x, (y + 1) % ys, z, core), at(x, (y + ys - 1) % ys, z, core))

    here = (x, y, z, core)
    rounds = [(place, size) for place, size in ((1, ys), (3, cores), (0, xs)) if size > 1]

    def along(place, size, distance):
        there = list(here)
        there[place] = (here[place] + distance) % size
        return at(*there)

    greeted = [along(place, size, d) for place, size in rounds for d in range(1, size)]

    rows = PIECE * SUBROWS
    parts = [pl.ds(k * rows, rows) for k in range(HELD)]
    loads = [
        pltpu.make_async_copy(source, target, local_sem.at[k])
        for k, (source, target) in enumerate(
            (
                (left_root, left),
                (right_root, right),
                (left_stats, new_left),
                (right_stats, new_right),
                (position_in, position),
                (owner_in, owner),
                (table_in, table),
                *((gradient.at[part], flat.at[part]) for part in parts),
            )
        )
    ]
    for k in (4, 5, 6, *range(7, 7 + HELD), 0, 1, 2, 3):
        loads[k].start()

    barrier = pltpu.get_barrier_semaphore()
    for device in greeted:
        pl.semaphore_signal(barrier, inc=1, device_id=device, device_id_type=MESH)
    planes = len(greeted)
    if zs > 1:
        planes += jnp.where(z == HUB, zs - 1, 1)

        @pl.when(z == HUB)
        def _():
            for d in range(1, zs):
                pl.semaphore_signal(barrier, inc=1, device_id=along(2, zs, d), device_id_type=MESH)

        @pl.when(z != HUB)
        def _():
            pl.semaphore_signal(
                barrier, inc=1, device_id=at(x, y, HUB, core), device_id_type=MESH
            )


    group = (dp * (xs * ys) + mp) // RING

    def find(b, found):
        place, device = position[b], owner[b]
        return tuple(
            jnp.where(place == GROUP_BLOCKS * group + k, device, f) for k, f in enumerate(found)
        )

    for k in (4, 5, 6):
        loads[k].wait()
    zero = jnp.int32(0)
    found = lax.fori_loop(0, position.shape[0], find, (zero,) * GROUP_BLOCKS)
    row = zero
    for f in found:
        row = row * RING + (f - RING * group)
    row = jnp.clip(row, 0, RING**GROUP_BLOCKS - 1)
    base = (row * RING + y) * WORDS
    words = [table[base + k] for k in range(7)]

    for k, part in enumerate(parts):
        loads[7 + k].wait()
        wide[part, :] = flat[part, :].astype(F32)

    def take(s):
        for k in range(HELD):
            for h in range(COLS // LANES):
                start = k * rows + s * (COLS // LANES) + h
                block = wide[pl.ds(start, PIECE, stride=SUBROWS), :]
                own[s][k, :, h * LANES : (h + 1) * LANES] = block.astype(BF16)

    def copy_of(out, into, send, recv, s, w, late):
        slots = pl.ds(w * SLOTS + late * EARLY, EARLY)
        return pltpu.make_async_remote_copy(
            src_ref=out[s].at[slots],
            dst_ref=into[s].at[slots],
            send_sem=send.at[s],
            recv_sem=recv.at[s, late],
            device_id=neighbours[w],
            device_id_type=MESH,
        )

    def both_came(out, into, send, recv, s, late):
        slots = pl.ds(0, 2 * EARLY)
        pltpu.make_async_remote_copy(
            src_ref=out[s].at[slots],
            dst_ref=into[s].at[slots],
            send_sem=send.at[s],
            recv_sem=recv.at[s, late],
            device_id=neighbours[0],
            device_id_type=MESH,
        ).wait_recv()

    def fill_own(out, source, pair, size, s, w):
        for t in range(EARLY):
            out[s][w * SLOTS + t] = source[s][jnp.minimum(code(pair[w], t), size - 1)]

    def send_own(out, into, send, recv, source, pair, size, s):
        for w in range(2):
            fill_own(out, source, pair, size, s, w)
            copy_of(out, into, send, recv, s, w, 0).start()

    def send_on(out, into, send, recv, source, pair, size, s):
        both_came(out, into, send, recv, s, 0)
        for w in range(2):
            for t in range(EARLY, SLOTS):
                c = code(pair[w], t)
                passed = into[s][w * SLOTS + t - EARLY]
                mine = source[s][jnp.minimum(c, size - 1)]
                out[s][w * SLOTS + t] = jnp.where(c == size, passed, mine)
            copy_of(out, into, send, recv, s, w, 1).start()

    def arrive(out, into, send, recv, s):
        both_came(out, into, send, recv, s, 1)

    def all_sent(out, into, send, recv, s):
        pltpu.make_async_remote_copy(
            src_ref=out[s],
            dst_ref=into[s],
            send_sem=send.at[s],
            recv_sem=recv.at[s, 0],
            device_id=neighbours[0],
            device_id_type=MESH,
        ).wait_send()

    def pick(source, into, c, size, s):
        mine = source[s][jnp.minimum(c, size - 1)]
        came = into[s][jnp.clip(c - size, 0, 2 * SLOTS - 1)]
        return jnp.where(c < size, mine, came)

    there = (there_out, there_in, there_send, there_recv)
    back = (back_out, back_in, back_send, back_recv)

    def there_own(s):
        take(s)
        send_own(*there, own, words[0:2], HELD, s)

    def there_on(s):
        send_on(*there, own, words[0:2], HELD, s)

    def assemble(s):
        arrive(*there, s)
        for q in range(OWNED):
            c = code(words[2 + q // 6], q % 6)
            value = pick(own, there_in, c, HELD, s)
            value = jnp.where(c < HELD + 2 * SLOTS, value, jnp.zeros_like(value))
            grads[s, pl.ds(q * PIECE, PIECE), :] = value

    def multiply_left(s):
        if s == 0:
            loads[0].wait()

        def tile(r, carry):
            at_rows = pl.ds(pl.multiple_of(r * COLS, COLS), COLS)
            roots = left[pl.ds(r * 2, 2)].reshape(COLS, B)
            part = jnp.dot(roots, grads[s], preferred_element_type=F32)
            half[at_rows, s * COLS : (s + 1) * COLS] = part.astype(BF16)
            return carry

        lax.fori_loop(0, B // COLS, tile, 0)

    def begin_right():
        loads[1].wait()

        def tile(r, carry):
            at_rows = pl.ds(pl.multiple_of(r * COLS, COLS), COLS)
            part = jnp.dot(
                half[at_rows, :EARLIER], right[:EARLIER, :COLS], preferred_element_type=F32
            )
            begun[pl.ds(r * 2, 2)] = part.reshape(2, PIECE, COLS)
            return carry

        lax.fori_loop(0, B // COLS, tile, 0)

    def back_first():
        last = QUARTERS - 1
        for t in range(EARLY):
            places = [jnp.minimum(code(words[4 + w], t), OWNED - 1) for w in range(2)]
            roots = jnp.concatenate([left[q] for q in places], axis=0)
            start = jnp.concatenate([begun[q] for q in places], axis=0)
            part = jnp.dot(roots, grads[last], preferred_element_type=F32).astype(BF16)
            part = jnp.dot(part, right[EARLIER:, :COLS], preferred_element_type=F32)
            part = (start + part).astype(BF16)
            for w in range(2):
                slot = w * SLOTS + t
                back_out[0][slot] = part[w * PIECE : (w + 1) * PIECE]
                pltpu.make_async_remote_copy(
                    src_ref=back_out[0].at[slot],
                    dst_ref=back_in[0].at[slot],
                    send_sem=back_send.at[0],
                    recv_sem=back_recv.at[0, 0],
                    device_id=neighbours[w],
                    device_id_type=MESH,
                ).start()

    take(0)
    for w in range(2):
        fill_own(there_out, own, words[0:2], HELD, 0, w)
    pl.semaphore_wait(barrier, planes)
    for w in range(2):
        copy_of(*there, 0, w, 0).start()
    there_own(1)
    there_own(2)
    grad_sum = jnp.zeros((8, LANES), F32)
    for part in parts:
        squares = jnp.square(wide[part, :])
        grad_sum += jnp.sum(squares.reshape(rows // 8, 8, LANES), axis=0)
    there_on(0)
    there_own(3)
    there_on(1)
    assemble(0)
    multiply_left(0)
    there_on(2)
    assemble(1)
    multiply_left(1)
    there_on(3)
    assemble(2)
    multiply_left(2)
    begin_right()
    assemble(3)
    back_first()
    multiply_left(3)

    def multiply_right(s, total):
        def tile(r, total):
            at_rows = pl.ds(pl.multiple_of(r * COLS, COLS), COLS)
            at_cols = pl.ds(s * COLS, COLS)
            if s == 0:
                part = jnp.dot(
                    half[at_rows, EARLIER:], right[EARLIER:, at_cols], preferred_element_type=F32
                )
                part = (begun[pl.ds(r * 2, 2)].reshape(COLS, COLS) + part).astype(BF16)
            else:
                part = jnp.dot(
                    half[at_rows, :], right[:, at_cols], preferred_element_type=F32
                ).astype(BF16)
            product[s][pl.ds(r * 2, 2)] = part.reshape(2, PIECE, COLS)
            squares = jnp.square(part.astype(F32))
            squares = squares[:, :LANES] + squares[:, LANES:]
            return total + jnp.sum(squares.reshape(COLS // 8, 8, LANES), axis=0)

        return lax.fori_loop(0, B // COLS, tile, total, unroll=True)

    def back_own(s):
        send_own(*back, product, words[4:6], OWNED, s)

    def back_on(s):
        send_on(*back, product, words[4:6], OWNED, s)

    def finish(s):
        arrive(*back, s)
        for k in range(HELD):
            value = pick(product, back_in, code(words[6], k), OWNED, s).astype(F32)
            for h in range(COLS // LANES):
                start = k * rows + s * (COLS // LANES) + h
                wide[pl.ds(start, PIECE, stride=SUBROWS), :] = value[:, h * LANES : (h + 1) * LANES]

    def exchange(r, d):
        place, size = rounds[r]
        return pltpu.make_async_remote_copy(
            src_ref=sums_out.at[r],
            dst_ref=sums_in.at[r, here[place]],
            send_sem=sums_send.at[r],
            recv_sem=sums_recv.at[r],
            device_id=along(place, size, d),
            device_id_type=MESH,
        )

    def exchange_start(r, sums):
        place, size = rounds[r]
        sums_out[r] = sums
        for d in range(1, size):
            exchange(r, d).start()

    def exchange_all(r):
        size = rounds[r][1]
        return pltpu.make_async_remote_copy(
            src_ref=sums_in.at[r, pl.ds(0, size - 1)],
            dst_ref=sums_in.at[r, pl.ds(0, size - 1)],
            send_sem=sums_send.at[r],
            recv_sem=sums_recv.at[r],
            device_id=along(*rounds[r], 1),
            device_id_type=MESH,
        )

    def exchange_end(r):
        place, size = rounds[r]
        sums_in[r, here[place]] = sums_out[r]
        exchange_all(r).wait_recv()
        return sum((sums_in[r, k] for k in range(1, size)), sums_in[r, 0])

    def exchange_sent(r):
        exchange_all(r).wait_send()

    gather, spread = len(rounds), len(rounds) + 1

    def plane_copy(r, source, target, device):
        return pltpu.make_async_remote_copy(
            src_ref=source,
            dst_ref=target,
            send_sem=sums_send.at[r],
            recv_sem=sums_recv.at[r],
            device_id=device,
            device_id_type=MESH,
        )

    def plane_all(r, count):
        part = sums_in.at[r, pl.ds(0, count)]
        return plane_copy(r, part, part, along(2, zs, 1))

    def planes_gather(sums):
        sums_out[gather] = sums

        @pl.when(z != HUB)
        def _():
            to = sums_in.at[gather, z]
            plane_copy(gather, sums_out.at[gather], to, at(x, y, HUB, core)).start()

    def planes_spread():
        @pl.when(z == HUB)
        def _():
            plane_all(gather, zs - 1).wait_recv()
            sums_in[gather, HUB] = sums_out[gather]
            total = sum((sums_in[gather, k] for k in range(1, zs)), sums_in[gather, 0])
            sums_out[spread] = total
            sums_in[spread, 0] = total
            for d in range(1, zs):
                to = sums_in.at[spread, 0]
                plane_copy(spread, sums_out.at[spread], to, along(2, zs, d)).start()

    def planes_end():
        @pl.when(z != HUB)
        def _():
            plane_all(spread, 1).wait_recv()

        return sums_in[spread, 0]

    def planes_sent():
        @pl.when(z == HUB)
        def _():
            plane_all(spread, zs - 1).wait_send()

        @pl.when(z != HUB)
        def _():
            plane_all(gather, 1).wait_send()

    factor = (1.0 - DECAY_RATE) / B

    def gram_left(r):
        if r == 0:
            loads[2].wait()
        at_rows = pl.ds(r * COLS, COLS)
        gram = jnp.zeros((COLS, B), F32)
        for s in range(QUARTERS):
            gram += lax.dot_general(
                grads[s, at_rows, :], grads[s], (((1,), (1,)), ((), ())), preferred_element_type=F32
            )
        new_left[at_rows, :] = DECAY_RATE * new_left[at_rows, :] + factor * gram

    def gram_right(r):
        if r == 0:
            loads[3].wait()
        at_rows = pl.ds(r * COLS, COLS)
        turned = grads[r].T
        for s in range(QUARTERS):
            at_cols = pl.ds(s * COLS, COLS)
            gram = jnp.dot(turned, grads[s], preferred_element_type=F32)
            new_right[at_rows, at_cols] = DECAY_RATE * new_right[at_rows, at_cols] + factor * gram

    direction_sum = jnp.zeros((8, LANES), F32)
    for s in range(QUARTERS - 1):
        direction_sum = multiply_right(s, direction_sum)
        if s > 0:
            back_own(s)
    direction_sum = multiply_right(QUARTERS - 1, direction_sum)
    exchange_start(0, jnp.concatenate([grad_sum, direction_sum], axis=0))
    back_on(0)
    back_own(QUARTERS - 1)
    gram_left(0)
    gram_left(1)
    back_on(1)
    gram_left(2)
    gram_left(3)
    back_on(2)
    rights = [functools.partial(gram_right, k) for k in range(4)]
    steps = [
        rights[0:2],
        rights[2:4] + [functools.partial(finish, 0), functools.partial(back_on, 3)],
        [],
    ]
    for r in range(len(rounds)):
        totals = exchange_end(r)
        if r + 1 < len(rounds):
            exchange_start(r + 1, totals)
        for step in steps[r]:
            step()
    for r in range(len(rounds), len(steps)):
        for step in steps[r]:
            step()
    if zs > 1:
        planes_gather(totals)
    finish(1)
    if zs > 1:
        planes_spread()
    for s in range(QUARTERS):
        all_sent(*there, s)
    for r in range(len(rounds)):
        exchange_sent(r)
    finish(2)
    if zs > 1:
        totals = planes_end()
        planes_sent()
    grad_total = jnp.sum(totals[0:8], keepdims=True)
    direction_total = jnp.sum(totals[8:16], keepdims=True)
    scale[...] = jnp.broadcast_to(jnp.sqrt(grad_total / (direction_total + EPSILON)), (8, LANES))
    finish(3)

    for s in range(QUARTERS):
        all_sent(*back, s)


def store(wide, scale, left, right, update, new_left, new_right, narrow, sem):
    copies = [
        pltpu.make_async_copy(left, new_left, sem.at[0]),
        pltpu.make_async_copy(right, new_right, sem.at[1]),
    ]
    for copy in copies:
        copy.start()
    rows = HELD * PIECE * SUBROWS // STORES
    for k in range(STORES):
        part = pl.ds(k * rows, rows)
        narrow[part, :] = (scale[0:1, :] * wide[part, :]).astype(BF16)
        copies.append(pltpu.make_async_copy(narrow.at[part], update.at[part], sem.at[2 + k]))
        copies[-1].start()
    for copy in copies:
        copy.wait()


def local(sizes, gradient, block_position, block_owner, left_stats, right_stats, left_root, right_root):
    xs, ys, zs, cores = sizes
    rounds = sum(size > 1 for size in sizes) + 1
    held_rows = HELD * PIECE * SUBROWS
    outside = pl.BlockSpec(memory_space=pltpu.HBM)
    inside = pl.BlockSpec(memory_space=pltpu.VMEM)

    def quarters(*lead):
        return [pltpu.VMEM((*lead, PIECE, COLS), BF16)] * QUARTERS

    dma = pltpu.SemaphoreType.DMA
    results = pl.pallas_call(
        functools.partial(kernel, sizes),
        out_shape=(
            pltpu.VMEM((held_rows, LANES), F32),
            pltpu.VMEM((8, LANES), F32),
            pltpu.VMEM((B, B), F32),
            pltpu.VMEM((B, B), F32),
        ),
        in_specs=[outside] * 8,
        out_specs=(inside,) * 4,
        scratch_shapes=[
            pltpu.SMEM(block_position.shape, jnp.int32),
            pltpu.SMEM(block_owner.shape, jnp.int32),
            pltpu.SMEM((RING**GROUP_BLOCKS * RING * WORDS,), jnp.int32),
            pltpu.VMEM((held_rows, LANES), BF16),
            pltpu.VMEM((QUARTERS, B, COLS), BF16),
            pltpu.VMEM((OWNED, PIECE, B), BF16),
            pltpu.VMEM((B, B), BF16),
            pltpu.VMEM((B, B), BF16),
            pltpu.VMEM((OWNED, PIECE, COLS), F32),
            quarters(HELD),
            quarters(2 * SLOTS),
            quarters(2 * SLOTS),
            quarters(OWNED),
            quarters(2 * SLOTS),
            quarters(2 * SLOTS),
            pltpu.VMEM((rounds, 16, LANES), F32),
            pltpu.VMEM((rounds, 4, 16, LANES), F32),
            dma((7 + HELD,)),
            dma((QUARTERS,)),
            dma((QUARTERS, 2)),
            dma((QUARTERS,)),
            dma((QUARTERS, 2)),
            dma((rounds,)),
            dma((rounds,)),
        ],
        compiler_params=pltpu.CompilerParams(
            collective_id=0, has_side_effects=True, vmem_limit_bytes=32 * 1024 * 1024
        ),
        name="shampoo",
    )(
        *(
            pltpu.with_memory_space_constraint(value, pltpu.HBM)
            for value in (
                block_position,
                block_owner,
                jnp.asarray(tables()),
                gradient.reshape(held_rows, LANES),
                left_stats[0],
                right_stats[0],
                left_root[0].reshape(OWNED, PIECE, B),
                right_root[0],
            )
        )
    )
    update, new_left, new_right = pl.pallas_call(
        store,
        out_shape=(
            jax.ShapeDtypeStruct((held_rows, LANES), BF16),
            jax.ShapeDtypeStruct((B, B), F32),
            jax.ShapeDtypeStruct((B, B), F32),
        ),
        in_specs=[inside] * 4,
        out_specs=(outside,) * 3,
        scratch_shapes=[pltpu.VMEM((held_rows, LANES), BF16), dma((2 + STORES,))],
        compiler_params=pltpu.CompilerParams(vmem_limit_bytes=4 * 1024 * 1024),
        name="store",
    )(*(pltpu.with_memory_space_constraint(value, pltpu.VMEM) for value in results))
    return (update.reshape(-1), new_left[None], new_right[None])


def solution(mesh):
    cores = 2
    sizes = (mesh.shape["mp"] // RING, RING, mesh.shape["dp"] // cores, cores)
    split = P(("dp", "mp"))
    slots = P(("dp", "mp"), None, None)
    return jax.shard_map(
        functools.partial(local, sizes),
        mesh=mesh,
        in_specs=(split, P(), P(), slots, slots, slots, slots),
        out_specs=(split, slots, slots),
        check_vma=False,
    )
```
